32 devices in a mesh: dp: 2 (over core), blk: 8 (over z, y), head: 2 (over x).
Axes of the slice: x: 2, y: 2, z: 4, core: 2. Of those that a mesh axis runs over, the one named last changes fastest.
Arguments:
- tokens: bfloat16 [4, 1024, 1024], P('dp', ('blk', 'head')), may hold values from -6 to 6
- w_qkv: bfloat16 [1024, 3072], P(('dp', 'blk'), 'head'), may hold values from -0.1875 to 0.1875
- w_out: bfloat16 [1024, 1024], P(('dp', 'blk'), 'head'), may hold values from -1.5 to 1.5
- w_up: bfloat16 [1024, 4096], P(('dp', 'blk'), 'head'), may hold values from -0.1875 to 0.1875
- w_down: bfloat16 [4096, 1024], P(('dp', 'blk'), 'head'), may hold values from -0.09375 to 0.09375
- gains: bfloat16 [2, 1024], P(None, ('dp', 'blk')), may hold values from 0.5 to 1.5
- biases: bfloat16 [6, 1024], P(None, ('dp', 'blk')), may hold values from -3 to 3
- up_bias: bfloat16 [4096], P(('dp', 'blk')), may hold values from -3 to 3
- lengths: int32 [4], P('dp'), may hold values from 256 to 1024, as said below
- cotangent: bfloat16 [4, 1024, 1024], P('dp', ('blk', 'head')), may hold values from -6 to 6
Outputs:
- output: bfloat16 [4, 1024, 1024], P('dp', ('blk', 'head'))
- grad_tokens: float32 [4, 1024, 1024], P('dp', ('blk', 'head'))
- grad_w_qkv: float32 [1024, 3072], P(('dp', 'blk'), 'head')
- grad_w_out: float32 [1024, 1024], P(('dp', 'blk'), 'head')
- grad_w_up: float32 [1024, 4096], P(('dp', 'blk'), 'head')
- grad_w_down: float32 [4096, 1024], P(('dp', 'blk'), 'head')
- grad_gains: float32 [2, 1024], P(None, ('dp', 'blk'))
- grad_biases: float32 [6, 1024], P(None, ('dp', 'blk'))
- grad_up_bias: float32 [4096], P(('dp', 'blk'))
The draws below stay inside these ranges and needn't reach their ends.
Inputs may be any that keep to these rules, and one draw needn't show every extreme that they name: `lengths`: in each group of 2 sequences that shares a dp index, one sequence, drawn from the seed, has all 1024 tokens.
All inputs are finite; a program needn't handle non-finite values.
Results may differ from the reference program's by a relative error of at most 0.012.
Values may be sent and summed in bfloat16 or wider, within the bound.
No kernel may reach another device: no remote copies, remote signals or barrier semaphores. Data moves between devices by JAX's collectives and lax.ppermute only.
A program may use at most 256 MiB of HBM per device.

```python
import jax
import jax.numpy as jnp
from jax import lax

D = 1024
HEADS = 16
HD = 64
FF = 4096
SEQ_DEV = 2
LEN = 1024
NSEQ = 4


def draw_lengths(key, part):
    key = jax.random.fold_in(key, 11)
    first_key, second_key = jax.random.split(key)
    group_count = NSEQ // SEQ_DEV
    random_lengths = jax.random.randint(first_key, (group_count, SEQ_DEV), LEN // 4, LEN + 1)
    chosen = jax.random.randint(second_key, (group_count, 1), 0, SEQ_DEV)
    is_full = jnp.arange(SEQ_DEV)[None, :] == chosen
    return jnp.where(is_full, LEN, random_lengths).reshape(NSEQ).astype(jnp.int32)


def raised(drawn, own_key, source, target, parts, factor):
    owner, partner = [(jnp.arange(drawn.shape[position]) // (drawn.shape[position] // parts)).reshape([-1 if axis == position else 1 for axis in range(drawn.ndim)]) for position in (source, target)]
    chosen = jax.random.permutation(own_key, parts)[partner]
    strong = (owner == chosen) | (owner == (partner + parts // 2) % parts)
    return jnp.where(strong, factor * drawn, drawn)


def block_scale(key, shape, cuts, least, largest):
    loudness, own = 1.0, jax.random.fold_in(key, 6)
    for dim, blocks in cuts:
        heights = jnp.exp(jax.random.uniform(jax.random.fold_in(own, dim), (blocks,), jnp.float32, least / len(cuts), largest / len(cuts)))
        loudness = loudness * jnp.repeat(heights, shape[dim] // blocks).reshape([-1 if axis == dim else 1 for axis in range(len(shape))])
    return loudness


def noise(own_key, shape, scale, reach, shards=(), kind=jnp.bfloat16):
    values = scale * jax.random.normal(own_key, shape, jnp.float32)
    if shards:
        values = values * block_scale(own_key, shape, shards, -0.22, 0.18)
    return jnp.clip(values, -reach, reach).astype(kind)


def heavy_noise(key, extent, scale, bound, cuts, heavy, held_as=jnp.bfloat16):
    array = scale * jax.random.normal(key, extent, jnp.float32)
    if cuts:
        array = array * block_scale(key, extent, cuts, -0.22, 0.18)
    return jnp.clip(raised(array, jax.random.fold_in(key, 3), *heavy), -bound, bound).astype(held_as)


def setup_inputs(seed: int = 0) -> dict:
    streams_of = jax.random.split(jax.random.key(seed), 11)
    return {
        "tokens": heavy_noise(streams_of[0], (NSEQ, LEN, D), 1.0, 6.0, ((0, 2), (1, 16)), (1, 2, 16, 2.0)),
        "w_qkv": noise(streams_of[1], (D, 3 * D), D ** -0.5, 0.1875, ((0, 16), (1, 2))),
        "w_out": noise(streams_of[2], (D, D), (max(1, D * 16 // LEN)) ** -0.5, 1.5, ((0, 16), (1, 2))),
        "w_up": noise(streams_of[3], (D, FF), D ** -0.5, 0.1875, ((0, 16), (1, 2))),
        "w_down": noise(streams_of[4], (FF, D), FF ** -0.5, 0.09375, ((0, 16), (1, 2))),
        "gains": jnp.clip(1.0 + 0.1 * jax.random.normal(streams_of[5], (2, D), jnp.float32), 0.5, 1.5).astype(jnp.bfloat16),
        "biases": noise(streams_of[6], (6, D), 0.5, 3.0, ((1, 16),)),
        "up_bias": noise(streams_of[7], (FF,), 0.5, 3.0, ((0, 16),)),
        "lengths": draw_lengths(jax.random.fold_in(streams_of[10], 71), 0),
        "cotangent": heavy_noise(streams_of[9], (NSEQ, LEN, D), 1.0, 6.0, ((0, 2), (1, 16)), (1, 2, 16, 2.0)),
    }


EPSILON = 1e-06
NEGATIVE = -1e+30

@jax.custom_vjp
def low(v):
    return lax.optimization_barrier(v.astype(jnp.bfloat16)).astype(jnp.float32)

@jax.custom_vjp
def low_back(v):
    return v

def low_keep(v):
    return (low(v), None)

def low_pass(kept, grad):
    return (grad,)

def back_keep(v):
    return (v, None)

def back_low(kept, grad):
    return (low(grad),)
low.defvjp(low_keep, low_pass)
low_back.defvjp(back_keep, back_low)

def highest_dot(left, right):
    return jnp.dot(left, right, precision=lax.Precision.HIGHEST)

def norm_rows(hidden, gain_vec, shift_vec):
    row_mean = lax.optimization_barrier(jnp.mean(hidden, axis=-1, keepdims=True))
    centred = hidden - row_mean
    spread = lax.optimization_barrier(jnp.mean(centred * centred, axis=-1, keepdims=True))
    return centred * lax.rsqrt(spread + EPSILON) * gain_vec + shift_vec

def reference(tokens, w_qkv, w_out, w_up, w_down, gains, biases, up_bias, lengths, cotangent):
    score_scale = HD ** (-0.5)
    positions = jnp.arange(LEN, dtype=jnp.int32)

    def forward(token_data, qkv_weight, out_weight, up_weight, down_weight, gain_rows, bias_rows, up_shift):
        qkv_shift = jnp.concatenate([bias_rows[0], jnp.zeros_like(bias_rows[0]), bias_rows[1]])

        def one_sequence(inputs):
            sequence, length = inputs
            projected_all = low(low_back(highest_dot(sequence, qkv_weight) + qkv_shift))
            queries = projected_all[:, :D].reshape(LEN, HEADS, HD)
            keys_all = projected_all[:, D:2 * D].reshape(LEN, HEADS, HD)
            values_all = projected_all[:, 2 * D:].reshape(LEN, HEADS, HD)
            raw_scores = jnp.einsum('qhd,khd->hqk', queries, keys_all, precision=lax.Precision.HIGHEST)
            scores = low_back(raw_scores * score_scale)
            scores = jnp.where((positions < length)[None, None, :], scores, NEGATIVE)
            row_max = lax.optimization_barrier(jnp.max(scores, axis=-1, keepdims=True))
            exp_scores = jnp.exp(scores - row_max)
            softmax_probs = exp_scores / lax.optimization_barrier(jnp.sum(exp_scores, axis=-1, keepdims=True))
            attended = jnp.einsum('hqk,khd->qhd', low(softmax_probs), values_all, precision=lax.Precision.HIGHEST)
            attended = low(low_back(attended.reshape(LEN, D)))
            projected = low_back(highest_dot(attended, out_weight) + bias_rows[2])
            normed = norm_rows(sequence + projected, gain_rows[0], bias_rows[3])
            pre_act = low_back(highest_dot(low(normed), up_weight) + up_shift)
            activated = low(jax.nn.gelu(pre_act, approximate=False))
            ffn_out = low_back(highest_dot(activated, down_weight) + bias_rows[4])
            return norm_rows(normed + ffn_out, gain_rows[1], bias_rows[5])
        return lax.map(jax.checkpoint(one_sequence), (token_data, lengths))
    params = (w_qkv, w_out, w_up, w_down, gains, biases, up_bias)
    params = tuple((entry.astype(jnp.float32) for entry in params))
    result, pullback = jax.vjp(forward, tokens.astype(jnp.float32), *params)
    grads = pullback(cotangent.astype(jnp.float32))
    return (result.astype(jnp.bfloat16), grads[0], grads[1], grads[2], grads[3], grads[4], grads[5], grads[6], grads[7])
```

```python
import jax
import jax.numpy as jnp
from jax import lax
from jax.sharding import PartitionSpec as P

HEADS = 16
HD = 64


EPSILON = 1e-06
NEGATIVE = -1e30


def norm_rows(hidden, gain_vec, shift_vec):
    row_mean = jnp.mean(hidden, axis=-1, keepdims=True)
    centred = hidden - row_mean
    spread = jnp.mean(centred * centred, axis=-1, keepdims=True)
    return centred * lax.rsqrt(spread + EPSILON) * gain_vec + shift_vec


def exact_gelu(values_in):
    return jax.nn.gelu(values_in, approximate=False)


def heads_of(array):
    return array.reshape(array.shape[0], -1, HD)


def masked_scores(query_block, key_block, key_mask, score_scale):
    raw_scores = (
        jnp.einsum("qhd,khd->hqk", query_block, key_block, preferred_element_type=jnp.float32)
        * score_scale
    )
    return jnp.where(key_mask[None, None, :], raw_scores, NEGATIVE)


def full_rows(query_block, key_block, key_mask, score_scale):
    scores = masked_scores(query_block, key_block, key_mask, score_scale)
    row_max = jnp.max(scores, axis=-1, keepdims=True)
    exp_scores = jnp.exp(scores - row_max)
    row_total = jnp.sum(exp_scores, axis=-1, keepdims=True)
    return (exp_scores / row_total, row_max, row_total)


def row_grads(query_block, key_block, value_block, grad_out, key_mask, score_scale):
    softmax_probs, row_max, row_total = full_rows(query_block, key_block, key_mask, score_scale)
    grad_probs = jnp.einsum(
        "qhd,khd->hqk", grad_out, value_block, preferred_element_type=jnp.float32
    )
    row_delta = jnp.sum(softmax_probs * grad_probs, axis=-1, keepdims=True)
    grad_scores = (softmax_probs * (grad_probs - row_delta)).astype(jnp.bfloat16)
    grad_query = (
        jnp.einsum("hqk,khd->qhd", grad_scores, key_block, preferred_element_type=jnp.float32)
        * score_scale
    )
    return (softmax_probs, grad_scores, grad_query, row_max + jnp.log(row_total), row_delta)


def on_device(tokens, w_qkv, w_out, w_up, w_down, gains, biases, up_bias, lengths, cotangent):
    sequences, local_len, width = tokens.shape
    groups = lax.axis_size("head")
    block_len = local_len * groups
    full_len = block_len * lax.axis_size("blk")
    lane_width = HEADS // groups * HD
    score_scale = HD ** (-0.5)
    part_qkv, part_out, part_up, part_down, gain_rows, bias_rows, up_shift = (
        lax.all_gather(w_qkv, ("dp", "blk"), axis=0, tiled=True),
        lax.all_gather(w_out, ("dp", "blk"), axis=0, tiled=True),
        lax.all_gather(w_up, ("dp", "blk"), axis=0, tiled=True),
        lax.all_gather(w_down, ("dp", "blk"), axis=0, tiled=True),
        lax.all_gather(gains, ("dp", "blk"), axis=1, tiled=True),
        lax.all_gather(biases, ("dp", "blk"), axis=1, tiled=True),
        lax.all_gather(up_bias, ("dp", "blk"), axis=0, tiled=True),
    )
    full_qkv, full_out, full_up, full_down = (
        lax.all_gather(part_qkv, "head", axis=1, tiled=True),
        lax.all_gather(part_out, "head", axis=1, tiled=True),
        lax.all_gather(part_up, "head", axis=1, tiled=True),
        lax.all_gather(part_down, "head", axis=1, tiled=True),
    )
    gain_float = gain_rows.astype(jnp.float32)
    bias_float = bias_rows.astype(jnp.float32)
    up_float = up_shift.astype(jnp.float32)
    token_rows = tokens.reshape(sequences * local_len, width)
    qkv_shift = jnp.concatenate([bias_float[0], jnp.zeros((width,), jnp.float32), bias_float[1]])
    projected_all = (
        jnp.dot(token_rows, full_qkv, preferred_element_type=jnp.float32) + qkv_shift
    ).astype(jnp.bfloat16)
    grouped = lax.all_to_all(
        projected_all.reshape(sequences, local_len, 3, groups, lane_width),
        "head",
        split_axis=3,
        concat_axis=1,
        tiled=True,
    )
    queries = grouped[:, :, 0, 0, :]
    key_pairs = grouped[:, :, 1:, 0, :]
    every_pair = lax.all_gather(key_pairs, "blk", axis=1, tiled=True)
    positions = jnp.arange(full_len, dtype=jnp.int32)
    key_valid = positions[None, :] < lengths[:, None]

    def attend(inputs):
        query_block, pair_block, key_mask = inputs
        softmax_probs, row_max, row_total = full_rows(
            heads_of(query_block), heads_of(pair_block[:, 0]), key_mask, score_scale
        )
        attended = jnp.einsum(
            "hqk,khd->qhd",
            softmax_probs.astype(jnp.bfloat16),
            heads_of(pair_block[:, 1]),
            preferred_element_type=jnp.float32,
        )
        return attended.reshape(-1, lane_width).astype(jnp.bfloat16)

    attended_all = lax.map(attend, (queries, every_pair, key_valid))
    returned = lax.all_to_all(
        attended_all[:, :, None, :], "head", split_axis=1, concat_axis=2, tiled=True
    )
    attn_rows = returned.reshape(sequences * local_len, width)
    projected = jnp.dot(attn_rows, full_out, preferred_element_type=jnp.float32) + bias_float[2]
    first_sum = token_rows.astype(jnp.float32) + projected
    normed, first_back = jax.vjp(norm_rows, first_sum, gain_float[0], bias_float[3])
    normed_low = normed.astype(jnp.bfloat16)
    pre_act = jnp.dot(normed_low, full_up, preferred_element_type=jnp.float32) + up_float
    activated, gelu_back = jax.vjp(exact_gelu, pre_act)
    activ_low = activated.astype(jnp.bfloat16)
    second_sum = (
        normed + jnp.dot(activ_low, full_down, preferred_element_type=jnp.float32) + bias_float[4]
    )
    result, second_back = jax.vjp(norm_rows, second_sum, gain_float[1], bias_float[5])
    output = result.astype(jnp.bfloat16).reshape(tokens.shape)
    grad_second, gain_grad_two, shift_grad_two = second_back(
        cotangent.reshape(-1, width).astype(jnp.float32)
    )
    grad_ffn = grad_second.astype(jnp.bfloat16)
    grad_down = jnp.dot(activ_low.T, grad_ffn, preferred_element_type=jnp.float32)
    shift_grad_down = jnp.sum(grad_ffn.astype(jnp.float32), axis=0)
    (grad_act,) = gelu_back(jnp.dot(grad_ffn, full_down.T, preferred_element_type=jnp.float32))
    grad_pre = grad_act.astype(jnp.bfloat16)
    grad_up = jnp.dot(normed_low.T, grad_pre, preferred_element_type=jnp.float32)
    grad_up_shift = jnp.sum(grad_pre.astype(jnp.float32), axis=0)
    grad_normed = grad_second + jnp.dot(grad_pre, full_up.T, preferred_element_type=jnp.float32)
    grad_first, gain_grad_one, shift_grad_one = first_back(grad_normed)
    grad_proj = grad_first.astype(jnp.bfloat16)
    grad_outw = jnp.dot(attn_rows.T, grad_proj, preferred_element_type=jnp.float32)
    shift_grad_out = jnp.sum(grad_proj.astype(jnp.float32), axis=0)
    grad_attn = jnp.dot(grad_proj, full_out.T, preferred_element_type=jnp.float32).astype(
        jnp.bfloat16
    )
    grad_grouped = lax.all_to_all(
        grad_attn.reshape(sequences, local_len, groups, lane_width),
        "head",
        split_axis=2,
        concat_axis=1,
        tiled=True,
    )
    grad_heads = grad_grouped[:, :, 0, :]

    def local_grads(inputs):
        query_block, pair_block, grad_block, key_mask = inputs
        query_heads = heads_of(query_block)
        grad_out = heads_of(grad_block)
        softmax_probs, grad_scores, grad_query, log_total, row_delta = row_grads(
            query_heads,
            heads_of(pair_block[:, 0]),
            heads_of(pair_block[:, 1]),
            grad_out,
            key_mask,
            score_scale,
        )
        grad_keys = (
            jnp.einsum("hqk,qhd->khd", grad_scores, query_heads, preferred_element_type=jnp.float32)
            * score_scale
        )
        grad_values = jnp.einsum(
            "hqk,qhd->khd",
            softmax_probs.astype(jnp.bfloat16),
            grad_out,
            preferred_element_type=jnp.float32,
        )
        key_terms = jnp.stack(
            [grad_keys.reshape(-1, lane_width), grad_values.reshape(-1, lane_width)], axis=1
        )
        return (grad_query.reshape(-1, lane_width).astype(jnp.bfloat16), key_terms)

    grad_queries, key_terms_all = lax.map(local_grads, (queries, every_pair, grad_heads, key_valid))
    grad_pairs = lax.psum_scatter(key_terms_all, "blk", scatter_dimension=1, tiled=True).astype(
        jnp.bfloat16
    )
    grad_mixed = jnp.concatenate([grad_queries[:, :, None, :], grad_pairs], axis=2)
    grad_back = lax.all_to_all(
        grad_mixed[:, :, :, None, :], "head", split_axis=1, concat_axis=3, tiled=True
    )
    grad_rows = grad_back.reshape(sequences * local_len, 3 * width)
    grad_qkv = jnp.dot(token_rows.T, grad_rows, preferred_element_type=jnp.float32)
    column_sums = jnp.sum(grad_rows.astype(jnp.float32), axis=0)
    grad_tokens = (
        grad_first + jnp.dot(grad_rows, full_qkv.T, preferred_element_type=jnp.float32)
    ).reshape(tokens.shape)
    gain_grads = jnp.stack([gain_grad_one, gain_grad_two])
    shift_grads = jnp.stack(
        [
            column_sums[:width],
            column_sums[2 * width :],
            shift_grad_out,
            shift_grad_one,
            shift_grad_down,
            shift_grad_two,
        ]
    )
    cols_qkv, cols_out, cols_up, cols_down = (
        lax.psum_scatter(grad_qkv, "head", scatter_dimension=1, tiled=True),
        lax.psum_scatter(grad_outw, "head", scatter_dimension=1, tiled=True),
        lax.psum_scatter(grad_up, "head", scatter_dimension=1, tiled=True),
        lax.psum_scatter(grad_down, "head", scatter_dimension=1, tiled=True),
    )
    share_qkv, share_out, share_up, share_down, share_gains, share_shifts, share_up_shift = (
        lax.psum_scatter(cols_qkv, ("dp", "blk"), scatter_dimension=0, tiled=True),
        lax.psum_scatter(cols_out, ("dp", "blk"), scatter_dimension=0, tiled=True),
        lax.psum_scatter(cols_up, ("dp", "blk"), scatter_dimension=0, tiled=True),
        lax.psum_scatter(cols_down, ("dp", "blk"), scatter_dimension=0, tiled=True),
        lax.psum_scatter(gain_grads, ("dp", "blk"), scatter_dimension=1, tiled=True),
        lax.psum_scatter(shift_grads, ("dp", "blk"), scatter_dimension=1, tiled=True),
        lax.psum_scatter(grad_up_shift, ("dp", "blk"), scatter_dimension=0, tiled=True),
    )
    total_gains, total_shifts, total_up_shift = lax.psum(
        (share_gains, share_shifts, share_up_shift), "head"
    )
    return (
        output,
        grad_tokens,
        share_qkv,
        share_out,
        share_up,
        share_down,
        total_gains,
        total_shifts,
        total_up_shift,
    )


SWAP = [(0, 1), (1, 0)]
PLANE = ("dp", "y", "head")
LINE = ("dp", "z")
OWNERS = ("dp", "z", "y")
EVERY = ("dp", "z", "y", "head")


def line_pairs(turn):
    return [
        (core * 4 + z, (z // 2) * 4 + 2 * core + (z + turn) % 2)
        for core in range(2)
        for z in range(4)
    ]


def to_planes(array, z_odd):
    first = jnp.where(z_odd, array[1], array[0])
    second = jnp.where(z_odd, array[0], array[1])
    return jnp.concatenate(
        [
            lax.ppermute(first, LINE, line_pairs(0)),
            lax.ppermute(second, LINE, line_pairs(1)),
        ]
    )


def from_planes(rows, z_odd):
    half = rows.shape[0] // 2
    first = lax.ppermute(rows[:half], LINE, [(to, src) for src, to in line_pairs(0)])
    second = lax.ppermute(rows[half:], LINE, [(to, src) for src, to in line_pairs(1)])
    return jnp.stack([jnp.where(z_odd, second, first), jnp.where(z_odd, first, second)])


def swap_x(array):
    return lax.ppermute(array, "head", SWAP)


def swap_y(array):
    return lax.ppermute(array, "y", SWAP)


def swap_xy(array):
    return lax.ppermute(array, ("y", "head"), [(i, 3 - i) for i in range(4)])


def swap_core(array):
    return lax.ppermute(array, "dp", SWAP)


def plane_gather(rows):
    return jnp.concatenate([rows, swap_x(rows), swap_y(rows), swap_xy(rows)])


def plane_sum(terms):
    own, for_x, for_y, for_xy = jnp.split(terms, 4)
    low = jnp.bfloat16
    return (
        own
        + swap_x(for_x.astype(low)).astype(jnp.float32)
        + swap_y(for_y.astype(low)).astype(jnp.float32)
        + swap_xy(for_xy.astype(low)).astype(jnp.float32)
    )


def in_order(flag, own, other):
    return jnp.stack([jnp.where(flag, other, own), jnp.where(flag, own, other)])


def turned(array, core, y, x):
    for axis, flag in ((0, core), (1, y), (2, x)):
        array = jnp.where(flag == 1, jnp.flip(array, axis), array)
    return array


def on_plane(tokens, w_qkv, w_out, w_up, w_down, gains, biases, up_bias, lengths, cotangent):
    sequences, local_len, width = tokens.shape
    rows = sequences * local_len
    low, full = jnp.bfloat16, jnp.float32
    core, z, y, x = (lax.axis_index(name) for name in EVERY)
    z_odd = z % 2 == 1
    score_scale = HD ** (-0.5)
    piece = HEADS * HD // 8
    own_d = w_qkv.shape[0]
    hidden_part = up_bias.shape[0]

    token_rows = to_planes(tokens, z_odd)

    groups = w_qkv.reshape(own_d, 3, 8, HD)
    came = swap_x(groups[:, 1])
    mine = jnp.stack(
        [
            jnp.where(x == 0, groups[:, 0], came),
            jnp.where(x == 0, groups[:, 2], groups[:, 0]),
            jnp.where(x == 0, came, groups[:, 2]),
        ],
        axis=1,
    ).reshape(own_d, 3, 2, 4 * HD)
    kept = lax.dynamic_index_in_dim(mine, y, 2, keepdims=False)
    given = lax.dynamic_index_in_dim(mine, 1 - y, 2, keepdims=False)
    both_rows = in_order(y == 1, kept, swap_y(given)).reshape(2 * own_d, 3 * 4 * HD)
    chip_qkv = lax.all_gather(both_rows, LINE, axis=0, tiled=True).reshape(width, 3, 2, piece)
    dev_qkv = lax.dynamic_index_in_dim(chip_qkv, core, 2, keepdims=False).reshape(width, 3 * piece)

    small = jnp.concatenate([gains.reshape(-1), biases.reshape(-1), up_bias])
    small_all = lax.all_gather(small, OWNERS).astype(full)
    vectors = small_all[:, : 8 * own_d].reshape(16, 8, own_d).transpose(1, 0, 2).reshape(8, width)
    gain_float, bias_float = vectors[:2], vectors[2:]
    up_parts = small_all[:, 8 * own_d :].reshape(2, 4, 2, hidden_part)
    up_float = lax.dynamic_index_in_dim(
        lax.dynamic_index_in_dim(up_parts, x, 0, keepdims=False), y, 1, keepdims=False
    ).reshape(4 * hidden_part)

    out_parts = lax.all_gather(w_out, EVERY)
    full_out = (
        out_parts.reshape(16, 2, own_d, width // 2).transpose(0, 2, 1, 3).reshape(width, width)
    )

    up_split = w_up.reshape(own_d, 4, 2, hidden_part)
    up_kept = lax.dynamic_index_in_dim(up_split, y, 2, keepdims=False)
    up_given = lax.dynamic_index_in_dim(up_split, 1 - y, 2, keepdims=False)
    up_rows = in_order(y == 1, up_kept, swap_y(up_given)).reshape(2 * own_d, 4 * hidden_part)
    dev_up = lax.all_gather(up_rows, LINE, axis=0, tiled=True)

    corner = [(0, 0), (1, 2), (2, 1), (3, 3)]
    down_rows = lax.ppermute(w_down, ("dp", "head"), corner)
    down_parts = lax.all_gather(down_rows, LINE).reshape(2, 4 * hidden_part, width // 2)
    dev_down = down_parts.transpose(1, 0, 2).reshape(4 * hidden_part, width)

    cotangent_rows = to_planes(cotangent, z_odd)
    other_lengths = swap_core(lengths)
    length = jnp.where(core == z // 2, lengths[z % 2], other_lengths[z % 2])

    core_rows = plane_gather(token_rows)
    all_rows = jnp.concatenate([core_rows, swap_core(core_rows)])

    first_col = (x * 8 + y * 4 + core * 2) * HD
    query_shift = lax.dynamic_slice_in_dim(bias_float[0], first_col, piece)
    value_shift = lax.dynamic_slice_in_dim(bias_float[1], first_col, piece)
    qkv_shift = jnp.concatenate([query_shift, jnp.zeros((piece,), full), value_shift])
    relative = (jnp.dot(all_rows, dev_qkv, preferred_element_type=full) + qkv_shift).astype(low)
    qkv = turned(relative.reshape(2, 2, 2, rows, 3 * piece), core, y, x).reshape(8 * rows, 3, piece)
    queries, keys, values = (heads_of(qkv[:, part]) for part in range(3))

    slot = jnp.arange(8, dtype=jnp.int32)
    slot_core, slot_y, slot_x = slot // 4, slot // 2 % 2, slot % 2
    turn = jnp.arange(2, dtype=jnp.int32)
    from_z = 2 * slot_core[:, None] + (z + turn[None, :]) % 2
    block = (from_z * 2 + slot_y[:, None]) * 2 + slot_x[:, None]
    positions = block[:, :, None] * local_len + jnp.arange(local_len, dtype=jnp.int32)
    key_valid = positions.reshape(-1) < length

    softmax_probs, _, _ = full_rows(queries, keys, key_valid, score_scale)
    attended = jnp.einsum(
        "hqk,khd->qhd", softmax_probs.astype(low), values, preferred_element_type=full
    ).astype(low)
    returned = lax.all_to_all(
        attended.reshape(8, rows, piece), PLANE, split_axis=0, concat_axis=0, tiled=True
    )
    attn_rows = (
        returned.reshape(2, 2, 2, rows, piece).transpose(3, 2, 1, 0, 4).reshape(rows, width)
    )
    projected = jnp.dot(attn_rows, full_out, preferred_element_type=full) + bias_float[2]
    first_sum = token_rows.astype(full) + projected
    normed, first_back = jax.vjp(norm_rows, first_sum, gain_float[0], bias_float[3])
    normed_all = plane_gather(normed.astype(low))
    pre_act = jnp.dot(normed_all, dev_up, preferred_element_type=full) + up_float
    activated, gelu_back = jax.vjp(exact_gelu, pre_act)
    activ_low = activated.astype(low)
    ffn_out = plane_sum(jnp.dot(activ_low, dev_down, preferred_element_type=full))
    second_sum = normed + ffn_out + bias_float[4]
    result, second_back = jax.vjp(norm_rows, second_sum, gain_float[1], bias_float[5])
    output = from_planes(result.astype(low), z_odd)
    grad_second, gain_grad_two, shift_grad_two = second_back(cotangent_rows.astype(full))
    grad_ffn = grad_second.astype(low)
    shift_grad_down = jnp.sum(grad_ffn.astype(full), axis=0)
    ffn_all = plane_gather(grad_ffn)
    (grad_act,) = gelu_back(jnp.dot(ffn_all, dev_down.T, preferred_element_type=full))
    grad_pre = grad_act.astype(low)
    grad_up_shift = jnp.sum(grad_pre.astype(full), axis=0)
    grad_normed = grad_second + plane_sum(jnp.dot(grad_pre, dev_up.T, preferred_element_type=full))

    grad_down = jnp.einsum(
        "th,tcd->chd",
        activ_low,
        ffn_all.reshape(4 * rows, 2, width // 2),
        preferred_element_type=full,
    ).astype(low)
    share_down = lax.psum_scatter(
        grad_down.reshape(8, hidden_part, width // 2), LINE, scatter_dimension=0, tiled=True
    ).reshape(hidden_part, width // 2)
    share_down = lax.ppermute(share_down, ("dp", "head"), corner).astype(full)
    grad_up = jnp.dot(normed_all.T, grad_pre, preferred_element_type=full).astype(low)
    share_up = lax.psum_scatter(grad_up, LINE, scatter_dimension=0, tiled=True)
    share_up = share_up.reshape(2, own_d, 4, hidden_part)
    up_home = lax.dynamic_index_in_dim(share_up, y, 0, keepdims=False)
    up_away = lax.dynamic_index_in_dim(share_up, 1 - y, 0, keepdims=False)
    share_up = (
        in_order(y == 1, up_home, swap_y(up_away))
        .transpose(1, 2, 0, 3)
        .reshape(own_d, 8 * hidden_part)
        .astype(full)
    )

    grad_first, gain_grad_one, shift_grad_one = first_back(grad_normed)
    grad_proj = grad_first.astype(low)
    shift_grad_out = jnp.sum(grad_proj.astype(full), axis=0)
    grad_attn = jnp.dot(grad_proj, full_out.T, preferred_element_type=full).astype(low)
    grad_out = lax.all_to_all(
        grad_attn.reshape(rows, 2, 2, 2, piece).transpose(3, 2, 1, 0, 4).reshape(8, rows, piece),
        PLANE,
        split_axis=0,
        concat_axis=0,
        tiled=True,
    )
    grad_outw = jnp.dot(attn_rows.T, grad_proj, preferred_element_type=full).astype(low)
    share_out = lax.psum_scatter(
        grad_outw.reshape(16, own_d, 2, width // 2)
        .transpose(0, 2, 1, 3)
        .reshape(32 * own_d, width // 2),
        EVERY,
        scatter_dimension=0,
        tiled=True,
    ).astype(full)

    grad_heads = heads_of(grad_out.reshape(8 * rows, piece))
    probs, grad_scores, grad_queries, _, _ = row_grads(
        queries, keys, values, grad_heads, key_valid, score_scale
    )
    grad_keys = (
        jnp.einsum("hqk,qhd->khd", grad_scores, queries, preferred_element_type=full) * score_scale
    )
    grad_values = jnp.einsum(
        "hqk,qhd->khd", probs.astype(low), grad_heads, preferred_element_type=full
    )
    grad_qkv = jnp.stack([grad_queries, grad_keys, grad_values], axis=1).astype(low)
    grad_qkv = turned(grad_qkv.reshape(2, 2, 2, rows, 3 * piece), core, y, x)
    grad_qkv = grad_qkv.reshape(8 * rows, 3 * piece)
    column_sums = jnp.sum(grad_qkv.astype(full), axis=0)

    back_terms = jnp.dot(grad_qkv, dev_qkv.T, preferred_element_type=full)
    core_terms = back_terms[: 4 * rows] + swap_core(back_terms[4 * rows :].astype(low)).astype(full)
    grad_rows = grad_first + plane_sum(core_terms)
    grad_tokens = from_planes(grad_rows.astype(low), z_odd).astype(full)

    grad_w = jnp.dot(all_rows.T, grad_qkv, preferred_element_type=full).astype(low)
    grad_w = lax.psum_scatter(
        grad_w.reshape(2, 4, 2 * own_d, 3, piece), "z", scatter_dimension=1, tiled=False
    )
    w_home = lax.dynamic_index_in_dim(grad_w, core, 0, keepdims=False)
    w_away = lax.dynamic_index_in_dim(grad_w, 1 - core, 0, keepdims=False)
    w_chip = in_order(core == 1, w_home, swap_core(w_away)).transpose(1, 2, 0, 3)
    w_chip = w_chip.reshape(2, own_d, 3, 2 * piece)
    y_home = lax.dynamic_index_in_dim(w_chip, y, 0, keepdims=False)
    y_away = lax.dynamic_index_in_dim(w_chip, 1 - y, 0, keepdims=False)
    w_half = in_order(y == 1, y_home, swap_y(y_away)).transpose(1, 2, 0, 3)
    w_half = w_half.reshape(own_d, 3, 4 * piece)
    crossed = swap_x(jnp.where(x == 0, w_half[:, 2], w_half[:, 0]))
    share_qkv = jnp.concatenate(
        [
            jnp.where(x == 0, w_half[:, 0], w_half[:, 1]),
            crossed,
            jnp.where(x == 0, w_half[:, 1], w_half[:, 2]),
        ],
        axis=1,
    ).astype(full)

    def placed(part):
        return lax.dynamic_update_slice_in_dim(jnp.zeros((width,), full), part, first_col, 0)

    vector_grads = jnp.stack(
        [
            gain_grad_one,
            gain_grad_two,
            placed(column_sums[:piece]),
            placed(column_sums[2 * piece :]),
            shift_grad_out,
            shift_grad_one,
            shift_grad_down,
            shift_grad_two,
        ]
    )
    vector_grads = vector_grads.reshape(8, 16, own_d).transpose(1, 0, 2).reshape(16, 8 * own_d)
    at_core = (jnp.arange(2) == x)[:, None, None, None]
    at_y = (jnp.arange(2) == y)[None, None, :, None]
    up_grads = jnp.where(at_core & at_y, grad_up_shift.reshape(1, 4, 1, hidden_part), 0.0)
    small_grads = jnp.concatenate([vector_grads, up_grads.reshape(16, hidden_part)], axis=1)
    small_grads = jnp.repeat(small_grads, 2, axis=0)
    small_back = lax.all_to_all(small_grads, EVERY, split_axis=0, concat_axis=0, tiled=True)
    small_total = jnp.sum(small_back, axis=0)
    vector_total = small_total[: 8 * own_d].reshape(8, own_d)
    return (
        output,
        grad_tokens,
        share_qkv,
        share_out,
        share_up,
        share_down,
        vector_total[:2],
        vector_total[2:],
        small_total[8 * own_d :],
    )


def fits_planes(mesh):
    return dict(mesh.shape) == {"dp": 2, "blk": 8, "head": 2}


def solution(mesh):
    if fits_planes(mesh):
        body = on_plane
        mesh = jax.sharding.Mesh(mesh.devices.reshape(2, 4, 2, 2), EVERY)
        blk = ("z", "y")
    else:
        body = on_device
        blk = ("blk",)
    token_spec = P("dp", (*blk, "head"), None)
    weight_spec = P(("dp", *blk), "head")
    vector_spec = P(None, ("dp", *blk))
    hidden_spec = P(("dp", *blk))
    return jax.shard_map(
        body,
        mesh=mesh,
        in_specs=(
            token_spec,
            *[weight_spec] * 4,
            vector_spec,
            vector_spec,
            hidden_spec,
            P("dp"),
            token_spec,
        ),
        out_specs=(
            token_spec,
            token_spec,
            *[weight_spec] * 4,
            vector_spec,
            vector_spec,
            hidden_spec,
        ),
        check_vma=False,
    )
```

```python
import jax
import jax.numpy as jnp
from jax import lax
from jax.sharding import PartitionSpec as P

HEADS = 16
HD = 64


EPSILON = 1e-06
NEGATIVE = -1e30


def norm_rows(hidden, gain_vec, shift_vec):
    row_mean = jnp.mean(hidden, axis=-1, keepdims=True)
    centred = hidden - row_mean
    spread = jnp.mean(centred * centred, axis=-1, keepdims=True)
    return centred * lax.rsqrt(spread + EPSILON) * gain_vec + shift_vec


def exact_gelu(values_in):
    return jax.nn.gelu(values_in, approximate=False)


def heads_of(array):
    return array.reshape(array.shape[0], -1, HD)


def masked_scores(query_block, key_block, key_mask, score_scale):
    raw_scores = (
        jnp.einsum("qhd,khd->hqk", query_block, key_block, preferred_element_type=jnp.float32)
        * score_scale
    )
    return jnp.where(key_mask[None, None, :], raw_scores, NEGATIVE)


def full_rows(query_block, key_block, key_mask, score_scale):
    scores = masked_scores(query_block, key_block, key_mask, score_scale)
    row_max = jnp.max(scores, axis=-1, keepdims=True)
    exp_scores = jnp.exp(scores - row_max)
    row_total = jnp.sum(exp_scores, axis=-1, keepdims=True)
    return (exp_scores / row_total, row_max, row_total)


def row_grads(query_block, key_block, value_block, grad_out, key_mask, score_scale):
    softmax_probs, row_max, row_total = full_rows(query_block, key_block, key_mask, score_scale)
    grad_probs = jnp.einsum(
        "qhd,khd->hqk", grad_out, value_block, preferred_element_type=jnp.float32
    )
    row_delta = jnp.sum(softmax_probs * grad_probs, axis=-1, keepdims=True)
    grad_scores = (softmax_probs * (grad_probs - row_delta)).astype(jnp.bfloat16)
    grad_query = (
        jnp.einsum("hqk,khd->qhd", grad_scores, key_block, preferred_element_type=jnp.float32)
        * score_scale
    )
    return (softmax_probs, grad_scores, grad_query, row_max + jnp.log(row_total), row_delta)


def on_device(tokens, w_qkv, w_out, w_up, w_down, gains, biases, up_bias, lengths, cotangent):
    sequences, local_len, width = tokens.shape
    groups = lax.axis_size("head")
    block_len = local_len * groups
    full_len = block_len * lax.axis_size("blk")
    lane_width = HEADS // groups * HD
    score_scale = HD ** (-0.5)
    part_qkv, part_out, part_up, part_down, gain_rows, bias_rows, up_shift = (
        lax.all_gather(w_qkv, ("dp", "blk"), axis=0, tiled=True),
        lax.all_gather(w_out, ("dp", "blk"), axis=0, tiled=True),
        lax.all_gather(w_up, ("dp", "blk"), axis=0, tiled=True),
        lax.all_gather(w_down, ("dp", "blk"), axis=0, tiled=True),
        lax.all_gather(gains, ("dp", "blk"), axis=1, tiled=True),
        lax.all_gather(biases, ("dp", "blk"), axis=1, tiled=True),
        lax.all_gather(up_bias, ("dp", "blk"), axis=0, tiled=True),
    )
    full_qkv, full_out, full_up, full_down = (
        lax.all_gather(part_qkv, "head", axis=1, tiled=True),
        lax.all_gather(part_out, "head", axis=1, tiled=True),
        lax.all_gather(part_up, "head", axis=1, tiled=True),
        lax.all_gather(part_down, "head", axis=1, tiled=True),
    )
    gain_float = gain_rows.astype(jnp.float32)
    bias_float = bias_rows.astype(jnp.float32)
    up_float = up_shift.astype(jnp.float32)
    token_rows = tokens.reshape(sequences * local_len, width)
    qkv_shift = jnp.concatenate([bias_float[0], jnp.zeros((width,), jnp.float32), bias_float[1]])
    projected_all = (
        jnp.dot(token_rows, full_qkv, preferred_element_type=jnp.float32) + qkv_shift
    ).astype(jnp.bfloat16)
    grouped = lax.all_to_all(
        projected_all.reshape(sequences, local_len, 3, groups, lane_width),
        "head",
        split_axis=3,
        concat_axis=1,
        tiled=True,
    )
    queries = grouped[:, :, 0, 0, :]
    key_pairs = grouped[:, :, 1:, 0, :]
    every_pair = lax.all_gather(key_pairs, "blk", axis=1, tiled=True)
    positions = jnp.arange(full_len, dtype=jnp.int32)
    key_valid = positions[None, :] < lengths[:, None]

    def attend(inputs):
        query_block, pair_block, key_mask = inputs
        softmax_probs, row_max, row_total = full_rows(
            heads_of(query_block), heads_of(pair_block[:, 0]), key_mask, score_scale
        )
        attended = jnp.einsum(
            "hqk,khd->qhd",
            softmax_probs.astype(jnp.bfloat16),
            heads_of(pair_block[:, 1]),
            preferred_element_type=jnp.float32,
        )
        return attended.reshape(-1, lane_width).astype(jnp.bfloat16)

    attended_all = lax.map(attend, (queries, every_pair, key_valid))
    returned = lax.all_to_all(
        attended_all[:, :, None, :], "head", split_axis=1, concat_axis=2, tiled=True
    )
    attn_rows = returned.reshape(sequences * local_len, width)
    projected = jnp.dot(attn_rows, full_out, preferred_element_type=jnp.float32) + bias_float[2]
    first_sum = token_rows.astype(jnp.float32) + projected
    normed, first_back = jax.vjp(norm_rows, first_sum, gain_float[0], bias_float[3])
    normed_low = normed.astype(jnp.bfloat16)
    pre_act = jnp.dot(normed_low, full_up, preferred_element_type=jnp.float32) + up_float
    activated, gelu_back = jax.vjp(exact_gelu, pre_act)
    activ_low = activated.astype(jnp.bfloat16)
    second_sum = (
        normed + jnp.dot(activ_low, full_down, preferred_element_type=jnp.float32) + bias_float[4]
    )
    result, second_back = jax.vjp(norm_rows, second_sum, gain_float[1], bias_float[5])
    output = result.astype(jnp.bfloat16).reshape(tokens.shape)
    grad_second, gain_grad_two, shift_grad_two = second_back(
        cotangent.reshape(-1, width).astype(jnp.float32)
    )
    grad_ffn = grad_second.astype(jnp.bfloat16)
    grad_down = jnp.dot(activ_low.T, grad_ffn, preferred_element_type=jnp.float32)
    shift_grad_down = jnp.sum(grad_ffn.astype(jnp.float32), axis=0)
    (grad_act,) = gelu_back(jnp.dot(grad_ffn, full_down.T, preferred_element_type=jnp.float32))
    grad_pre = grad_act.astype(jnp.bfloat16)
    grad_up = jnp.dot(normed_low.T, grad_pre, preferred_element_type=jnp.float32)
    grad_up_shift = jnp.sum(grad_pre.astype(jnp.float32), axis=0)
    grad_normed = grad_second + jnp.dot(grad_pre, full_up.T, preferred_element_type=jnp.float32)
    grad_first, gain_grad_one, shift_grad_one = first_back(grad_normed)
    grad_proj = grad_first.astype(jnp.bfloat16)
    grad_outw = jnp.dot(attn_rows.T, grad_proj, preferred_element_type=jnp.float32)
    shift_grad_out = jnp.sum(grad_proj.astype(jnp.float32), axis=0)
    grad_attn = jnp.dot(grad_proj, full_out.T, preferred_element_type=jnp.float32).astype(
        jnp.bfloat16
    )
    grad_grouped = lax.all_to_all(
        grad_attn.reshape(sequences, local_len, groups, lane_width),
        "head",
        split_axis=2,
        concat_axis=1,
        tiled=True,
    )
    grad_heads = grad_grouped[:, :, 0, :]

    def local_grads(inputs):
        query_block, pair_block, grad_block, key_mask = inputs
        query_heads = heads_of(query_block)
        grad_out = heads_of(grad_block)
        softmax_probs, grad_scores, grad_query, log_total, row_delta = row_grads(
            query_heads,
            heads_of(pair_block[:, 0]),
            heads_of(pair_block[:, 1]),
            grad_out,
            key_mask,
            score_scale,
        )
        grad_keys = (
            jnp.einsum("hqk,qhd->khd", grad_scores, query_heads, preferred_element_type=jnp.float32)
            * score_scale
        )
        grad_values = jnp.einsum(
            "hqk,qhd->khd",
            softmax_probs.astype(jnp.bfloat16),
            grad_out,
            preferred_element_type=jnp.float32,
        )
        key_terms = jnp.stack(
            [grad_keys.reshape(-1, lane_width), grad_values.reshape(-1, lane_width)], axis=1
        )
        return (grad_query.reshape(-1, lane_width).astype(jnp.bfloat16), key_terms)

    grad_queries, key_terms_all = lax.map(local_grads, (queries, every_pair, grad_heads, key_valid))
    grad_pairs = lax.psum_scatter(key_terms_all, "blk", scatter_dimension=1, tiled=True).astype(
        jnp.bfloat16
    )
    grad_mixed = jnp.concatenate([grad_queries[:, :, None, :], grad_pairs], axis=2)
    grad_back = lax.all_to_all(
        grad_mixed[:, :, :, None, :], "head", split_axis=1, concat_axis=3, tiled=True
    )
    grad_rows = grad_back.reshape(sequences * local_len, 3 * width)
    grad_qkv = jnp.dot(token_rows.T, grad_rows, preferred_element_type=jnp.float32)
    column_sums = jnp.sum(grad_rows.astype(jnp.float32), axis=0)
    grad_tokens = (
        grad_first + jnp.dot(grad_rows, full_qkv.T, preferred_element_type=jnp.float32)
    ).reshape(tokens.shape)
    gain_grads = jnp.stack([gain_grad_one, gain_grad_two])
    shift_grads = jnp.stack(
        [
            column_sums[:width],
            column_sums[2 * width :],
            shift_grad_out,
            shift_grad_one,
            shift_grad_down,
            shift_grad_two,
        ]
    )
    cols_qkv, cols_out, cols_up, cols_down = (
        lax.psum_scatter(grad_qkv, "head", scatter_dimension=1, tiled=True),
        lax.psum_scatter(grad_outw, "head", scatter_dimension=1, tiled=True),
        lax.psum_scatter(grad_up, "head", scatter_dimension=1, tiled=True),
        lax.psum_scatter(grad_down, "head", scatter_dimension=1, tiled=True),
    )
    share_qkv, share_out, share_up, share_down, share_gains, share_shifts, share_up_shift = (
        lax.psum_scatter(cols_qkv, ("dp", "blk"), scatter_dimension=0, tiled=True),
        lax.psum_scatter(cols_out, ("dp", "blk"), scatter_dimension=0, tiled=True),
        lax.psum_scatter(cols_up, ("dp", "blk"), scatter_dimension=0, tiled=True),
        lax.psum_scatter(cols_down, ("dp", "blk"), scatter_dimension=0, tiled=True),
        lax.psum_scatter(gain_grads, ("dp", "blk"), scatter_dimension=1, tiled=True),
        lax.psum_scatter(shift_grads, ("dp", "blk"), scatter_dimension=1, tiled=True),
        lax.psum_scatter(grad_up_shift, ("dp", "blk"), scatter_dimension=0, tiled=True),
    )
    total_gains, total_shifts, total_up_shift = lax.psum(
        (share_gains, share_shifts, share_up_shift), "head"
    )
    return (
        output,
        grad_tokens,
        share_qkv,
        share_out,
        share_up,
        share_down,
        total_gains,
        total_shifts,
        total_up_shift,
    )


SWAP = [(0, 1), (1, 0)]
PLANE = ("dp", "y", "head")
LINE = ("dp", "z")
OWNERS = ("dp", "z", "y")
EVERY = ("dp", "z", "y", "head")


def line_pairs(turn):
    return [
        (core * 4 + z, (z // 2) * 4 + 2 * core + (z + turn) % 2)
        for core in range(2)
        for z in range(4)
    ]


def to_planes(array, z_odd):
    first = jnp.where(z_odd, array[1], array[0])
    second = jnp.where(z_odd, array[0], array[1])
    return jnp.concatenate(
        [
            lax.ppermute(first, LINE, line_pairs(0)),
            lax.ppermute(second, LINE, line_pairs(1)),
        ]
    )


def from_planes(rows, z_odd):
    half = rows.shape[0] // 2
    first = lax.ppermute(rows[:half], LINE, [(to, src) for src, to in line_pairs(0)])
    second = lax.ppermute(rows[half:], LINE, [(to, src) for src, to in line_pairs(1)])
    return jnp.stack([jnp.where(z_odd, second, first), jnp.where(z_odd, first, second)])


def swap_x(array):
    return lax.ppermute(array, "head", SWAP)


def swap_y(array):
    return lax.ppermute(array, "y", SWAP)


def swap_xy(array):
    return lax.ppermute(array, ("y", "head"), [(i, 3 - i) for i in range(4)])


def swap_core(array):
    return lax.ppermute(array, "dp", SWAP)


def plane_gather(rows):
    return jnp.concatenate([rows, swap_x(rows), swap_y(rows), swap_xy(rows)])


def plane_sum(terms):
    own, for_x, for_y, for_xy = jnp.split(terms, 4)
    low = jnp.bfloat16
    return (
        own
        + swap_x(for_x.astype(low)).astype(jnp.float32)
        + swap_y(for_y.astype(low)).astype(jnp.float32)
        + swap_xy(for_xy.astype(low)).astype(jnp.float32)
    )


def in_order(flag, own, other):
    return jnp.stack([jnp.where(flag, other, own), jnp.where(flag, own, other)])


def turned(array, core, y, x):
    for axis, flag in ((0, core), (1, y), (2, x)):
        array = jnp.where(flag == 1, jnp.flip(array, axis), array)
    return array


def rotated(array, distance):
    return lax.ppermute(array, "z", [(i, (i + distance) % 4) for i in range(4)])


def z_sum(parts, z, axis):
    total = lax.dynamic_index_in_dim(parts, z, axis, keepdims=False)
    for distance in (1, 2, 3):
        sent = lax.dynamic_index_in_dim(parts, (z + distance) % 4, axis, keepdims=False)
        total = total + rotated(sent.astype(jnp.bfloat16), distance).astype(jnp.float32)
    return total


def core_sum(parts, core):
    own = lax.dynamic_index_in_dim(parts, core, 0, keepdims=False)
    sent = lax.dynamic_index_in_dim(parts, 1 - core, 0, keepdims=False)
    return own + swap_core(sent.astype(jnp.bfloat16)).astype(jnp.float32)


def on_plane(tokens, w_qkv, w_out, w_up, w_down, gains, biases, up_bias, lengths, cotangent):
    sequences, local_len, width = tokens.shape
    rows = sequences * local_len
    low, full = jnp.bfloat16, jnp.float32
    core, z, y, x = (lax.axis_index(name) for name in EVERY)
    z_odd = z % 2 == 1
    score_scale = HD ** (-0.5)
    piece = HEADS * HD // 8
    own_d = w_qkv.shape[0]
    hidden_part = up_bias.shape[0]

    token_rows = to_planes(tokens, z_odd)

    groups = w_qkv.reshape(own_d, 3, 4 * piece)
    came = swap_x(groups[:, 1])
    mine = jnp.stack(
        [
            jnp.where(x == 0, groups[:, 0], came),
            jnp.where(x == 0, groups[:, 2], groups[:, 0]),
            jnp.where(x == 0, came, groups[:, 2]),
        ],
        axis=1,
    ).reshape(own_d, 3, 2, 2, piece)
    coded = jnp.concatenate([lengths // 128, lengths % 128]).astype(low)
    small = jnp.concatenate([gains.reshape(-1), biases.reshape(-1), up_bias, coded])
    extra = jnp.pad(small, (0, 8 * 3 * piece - small.shape[0])).reshape(8, 3 * piece)
    shares = jnp.concatenate(
        [
            mine.transpose(2, 3, 0, 1, 4).reshape(2, 2, own_d, 3 * piece),
            jnp.broadcast_to(extra, (2, 2, 8, 3 * piece)),
        ],
        axis=2,
    )
    y_kept = lax.dynamic_index_in_dim(shares, y, 0, keepdims=False)
    y_given = lax.dynamic_index_in_dim(shares, 1 - y, 0, keepdims=False)
    shares = in_order(y == 1, y_kept, swap_y(y_given))
    core_kept = lax.dynamic_index_in_dim(shares, core, 1, keepdims=False)
    core_given = lax.dynamic_index_in_dim(shares, 1 - core, 1, keepdims=False)
    shares = in_order(core == 1, core_kept, swap_core(core_given))
    gathered = jnp.zeros((2, 4, 2, own_d + 8, 3 * piece), low)
    gathered = lax.dynamic_update_index_in_dim(gathered, shares, z, 1)
    for distance in (1, 2, 3):
        gathered = lax.dynamic_update_index_in_dim(
            gathered, rotated(shares, distance), (z - distance) % 4, 1
        )
    dev_qkv = gathered[:, :, :, :own_d].reshape(width, 3 * piece)
    small_all = gathered[:, :, :, own_d:].reshape(16, 8 * 3 * piece).astype(full)
    vectors = small_all[:, : 8 * own_d].reshape(16, 8, own_d).transpose(1, 0, 2).reshape(8, width)
    gain_float, bias_float = vectors[:2], vectors[2:]
    up_parts = small_all[:, 8 * own_d : 8 * own_d + hidden_part].reshape(2, 4, 2, hidden_part)
    up_float = lax.dynamic_index_in_dim(
        lax.dynamic_index_in_dim(up_parts, x, 0, keepdims=False), y, 1, keepdims=False
    ).reshape(4 * hidden_part)
    code = small_all[z // 2 * 8, 8 * own_d + hidden_part :][:4]
    length = (code[z % 2] * 128 + code[2 + z % 2]).astype(jnp.int32)

    out_parts = lax.all_gather(w_out, EVERY)
    full_out = (
        out_parts.reshape(16, 2, own_d, width // 2).transpose(0, 2, 1, 3).reshape(width, width)
    )

    up_split = w_up.reshape(own_d, 4, 2, hidden_part)
    up_kept = lax.dynamic_index_in_dim(up_split, y, 2, keepdims=False)
    up_given = lax.dynamic_index_in_dim(up_split, 1 - y, 2, keepdims=False)
    up_rows = in_order(y == 1, up_kept, swap_y(up_given)).reshape(2 * own_d, 4 * hidden_part)
    up_rows, out_parts = lax.optimization_barrier((up_rows, out_parts))
    dev_up = lax.all_gather(up_rows, LINE, axis=0, tiled=True)

    corner = [(0, 0), (1, 2), (2, 1), (3, 3)]
    down_rows = lax.ppermute(w_down, ("dp", "head"), corner)
    down_rows, dev_up = lax.optimization_barrier((down_rows, dev_up))
    down_parts = lax.all_gather(down_rows, LINE).reshape(2, 4 * hidden_part, width // 2)
    dev_down = down_parts.transpose(1, 0, 2).reshape(4 * hidden_part, width)

    cotangent_rows = to_planes(cotangent, z_odd)

    core_rows = plane_gather(token_rows)
    all_rows = jnp.concatenate([core_rows, swap_core(core_rows)])

    first_col = (x * 8 + y * 4 + core * 2) * HD
    query_shift = lax.dynamic_slice_in_dim(bias_float[0], first_col, piece)
    value_shift = lax.dynamic_slice_in_dim(bias_float[1], first_col, piece)
    qkv_shift = jnp.concatenate([query_shift, jnp.zeros((piece,), full), value_shift])
    relative = (jnp.dot(all_rows, dev_qkv, preferred_element_type=full) + qkv_shift).astype(low)
    qkv = turned(relative.reshape(2, 2, 2, rows, 3 * piece), core, y, x).reshape(8 * rows, 3, piece)
    queries, keys, values = (heads_of(qkv[:, part]) for part in range(3))

    slot = jnp.arange(8, dtype=jnp.int32)
    slot_core, slot_y, slot_x = slot // 4, slot // 2 % 2, slot % 2
    turn = jnp.arange(2, dtype=jnp.int32)
    from_z = 2 * slot_core[:, None] + (z + turn[None, :]) % 2
    block = (from_z * 2 + slot_y[:, None]) * 2 + slot_x[:, None]
    positions = block[:, :, None] * local_len + jnp.arange(local_len, dtype=jnp.int32)
    key_valid = positions.reshape(-1) < length

    softmax_probs, _, _ = full_rows(queries, keys, key_valid, score_scale)
    attended = jnp.einsum(
        "hqk,khd->qhd", softmax_probs.astype(low), values, preferred_element_type=full
    ).astype(low)
    returned = lax.all_to_all(
        attended.reshape(8, rows, piece), PLANE, split_axis=0, concat_axis=0, tiled=True
    )
    attn_rows = (
        returned.reshape(2, 2, 2, rows, piece).transpose(3, 2, 1, 0, 4).reshape(rows, width)
    )
    projected = jnp.dot(attn_rows, full_out, preferred_element_type=full) + bias_float[2]
    first_sum = token_rows.astype(full) + projected
    normed, first_back = jax.vjp(norm_rows, first_sum, gain_float[0], bias_float[3])

    swaps = (swap_x, swap_y, swap_xy)
    normed_low = normed.astype(low)
    normed_parts = [normed_low] + [swap(normed_low) for swap in swaps]
    activ_parts, gelu_backs, ffn_terms = [], [], []
    for part in normed_parts:
        pre_act = jnp.dot(part, dev_up, preferred_element_type=full) + up_float
        activated, gelu_back = jax.vjp(exact_gelu, pre_act)
        activ_parts.append(activated.astype(low))
        gelu_backs.append(gelu_back)
        ffn_terms.append(jnp.dot(activ_parts[-1], dev_down, preferred_element_type=full))
    ffn_out = ffn_terms[0]
    for swap, term in zip(swaps, ffn_terms[1:]):
        ffn_out = ffn_out + swap(term.astype(low)).astype(full)
    second_sum = normed + ffn_out + bias_float[4]
    result, second_back = jax.vjp(norm_rows, second_sum, gain_float[1], bias_float[5])
    output = from_planes(result.astype(low), z_odd)
    grad_second, gain_grad_two, shift_grad_two = second_back(cotangent_rows.astype(full))
    grad_ffn = grad_second.astype(low)
    shift_grad_down = jnp.sum(grad_ffn.astype(full), axis=0)

    ffn_parts = [grad_ffn] + [swap(grad_ffn) for swap in swaps]
    pre_parts, back_terms = [], []
    for part, gelu_back in zip(ffn_parts, gelu_backs):
        (grad_act,) = gelu_back(jnp.dot(part, dev_down.T, preferred_element_type=full))
        pre_parts.append(grad_act.astype(low))
        back_terms.append(jnp.dot(pre_parts[-1], dev_up.T, preferred_element_type=full))
    back_sent = [swap(term.astype(low)) for swap, term in zip(swaps, back_terms[1:])]

    ffn_all = jnp.concatenate(ffn_parts)
    activ_all = jnp.concatenate(activ_parts)
    grad_down = jnp.einsum(
        "th,tcd->chd",
        activ_all,
        ffn_all.reshape(4 * rows, 2, width // 2),
        preferred_element_type=full,
    )
    grad_down = core_sum(grad_down, core)
    back_sent, grad_down = lax.optimization_barrier((back_sent, grad_down))
    grad_normed = grad_second + back_terms[0]
    for sent in back_sent:
        grad_normed = grad_normed + sent.astype(full)
    share_down = z_sum(grad_down.reshape(4, hidden_part, width // 2), z, 0)
    share_down = lax.ppermute(share_down.astype(low), ("dp", "head"), corner).astype(full)

    pre_all = jnp.concatenate(pre_parts)
    normed_all = jnp.concatenate(normed_parts)
    grad_up_shift = jnp.sum(pre_all.astype(full), axis=0)
    grad_up = jnp.dot(normed_all.T, pre_all, preferred_element_type=full)
    grad_up = core_sum(grad_up.reshape(2, 8 * own_d, 4 * hidden_part), core)

    grad_first, gain_grad_one, shift_grad_one = first_back(grad_normed)
    grad_proj = grad_first.astype(low)
    shift_grad_out = jnp.sum(grad_proj.astype(full), axis=0)
    grad_attn = jnp.dot(grad_proj, full_out.T, preferred_element_type=full).astype(low)
    grad_out = lax.all_to_all(
        grad_attn.reshape(rows, 2, 2, 2, piece).transpose(3, 2, 1, 0, 4).reshape(8, rows, piece),
        PLANE,
        split_axis=0,
        concat_axis=0,
        tiled=True,
    )
    grad_out, grad_up = lax.optimization_barrier((grad_out, grad_up))
    share_up = z_sum(grad_up.reshape(4, 2 * own_d, 4 * hidden_part), z, 0).astype(low)
    share_up = share_up.reshape(2, own_d, 4, hidden_part)
    up_home = lax.dynamic_index_in_dim(share_up, y, 0, keepdims=False)
    up_away = lax.dynamic_index_in_dim(share_up, 1 - y, 0, keepdims=False)
    share_up = (
        in_order(y == 1, up_home, swap_y(up_away))
        .transpose(1, 2, 0, 3)
        .reshape(own_d, 8 * hidden_part)
        .astype(full)
    )

    grad_outw = jnp.dot(attn_rows.T, grad_proj, preferred_element_type=full)
    grad_outw = core_sum(grad_outw.reshape(2, 4, 2, own_d, width), core)
    out_home = lax.dynamic_index_in_dim(grad_outw, y, 1, keepdims=False)
    out_away = lax.dynamic_index_in_dim(grad_outw, 1 - y, 1, keepdims=False)
    grad_outw = out_home + swap_y(out_away.astype(low)).astype(full)
    grad_outw = grad_outw.reshape(4, own_d, 2, width // 2)
    out_home = lax.dynamic_index_in_dim(grad_outw, x, 2, keepdims=False)
    out_away = lax.dynamic_index_in_dim(grad_outw, 1 - x, 2, keepdims=False)
    grad_outw = out_home + swap_x(out_away.astype(low)).astype(full)
    share_out = z_sum(grad_outw, z, 0)

    vector_grads = jnp.stack(
        [
            gain_grad_one,
            gain_grad_two,
            shift_grad_out,
            shift_grad_one,
            shift_grad_down,
            shift_grad_two,
        ]
    )
    vector_grads = vector_grads.reshape(6, 16, own_d).transpose(1, 0, 2).reshape(16, 6 * own_d)
    at_core = (jnp.arange(2) == x)[:, None, None, None]
    at_y = (jnp.arange(2) == y)[None, None, :, None]
    up_grads = jnp.where(at_core & at_y, grad_up_shift.reshape(1, 4, 1, hidden_part), 0.0)
    small_grads = jnp.concatenate([vector_grads, up_grads.reshape(16, hidden_part)], axis=1)
    small_grads = jnp.repeat(small_grads, 2, axis=0)
    small_back = lax.all_to_all(small_grads, EVERY, split_axis=0, concat_axis=0, tiled=True)
    small_total = jnp.sum(small_back, axis=0)

    grad_heads = heads_of(grad_out.reshape(8 * rows, piece))
    probs, grad_scores, grad_queries, _, _ = row_grads(
        queries, keys, values, grad_heads, key_valid, score_scale
    )
    grad_keys = (
        jnp.einsum("hqk,qhd->khd", grad_scores, queries, preferred_element_type=full) * score_scale
    )
    grad_values = jnp.einsum(
        "hqk,qhd->khd", probs.astype(low), grad_heads, preferred_element_type=full
    )
    grad_qkv = jnp.stack([grad_queries, grad_keys, grad_values], axis=1).astype(low)
    grad_qkv = turned(grad_qkv.reshape(2, 2, 2, rows, 3 * piece), core, y, x)
    grad_qkv = grad_qkv.reshape(8 * rows, 3 * piece)
    column_sums = jnp.sum(grad_qkv.astype(full), axis=0)

    back_terms = jnp.dot(grad_qkv, dev_qkv.T, preferred_element_type=full)
    core_terms = back_terms[: 4 * rows] + swap_core(back_terms[4 * rows :].astype(low)).astype(full)
    grad_rows = grad_first + plane_sum(core_terms)
    grad_tokens = from_planes(grad_rows.astype(low), z_odd).astype(full)

    grad_w = jnp.dot(all_rows.T, grad_qkv, preferred_element_type=full)
    grad_w = z_sum(grad_w.reshape(2, 4, 2, own_d, 3 * piece), z, 1).astype(low)
    sent = jnp.stack([grad_w[..., : 2 * piece], grad_w[..., piece:]], axis=2)
    back = lax.all_to_all(
        sent.reshape(8, own_d, 2 * piece), PLANE, split_axis=0, concat_axis=0, tiled=True
    )
    back = back.reshape(2, 2, 2, own_d, 2, piece).transpose(3, 4, 2, 1, 0, 5)
    back = back.reshape(own_d, 2, 2, 4 * piece)
    share_qkv = jnp.concatenate(
        [
            jnp.where(x == 0, back[:, 0, 0], back[:, 0, 1]),
            jnp.where(x == 0, back[:, 0, 1], back[:, 1, 0]),
            jnp.where(x == 0, back[:, 1, 0], back[:, 1, 1]),
        ],
        axis=1,
    ).astype(full)

    late = jnp.stack([column_sums[:piece], column_sums[2 * piece :]]).reshape(2, 2, own_d)
    late = late.transpose(1, 0, 2).reshape(1, 1, 2, 1, 2 * own_d)
    at_z = (jnp.arange(4) == 2 * y + core)[None, :, None, None, None]
    late = jnp.where(at_core[..., None] & at_z, late, 0.0)
    late = jnp.broadcast_to(late, (2, 4, 2, 2, 2 * own_d)).reshape(32, 2 * own_d)
    late_back = lax.all_to_all(late, EVERY, split_axis=0, concat_axis=0, tiled=True)
    late_total = jnp.sum(late_back, axis=0).reshape(2, own_d)
    vector_total = small_total[: 6 * own_d].reshape(6, own_d)
    return (
        output,
        grad_tokens,
        share_qkv,
        share_out,
        share_up,
        share_down,
        vector_total[:2],
        jnp.concatenate([late_total, vector_total[2:]]),
        small_total[6 * own_d :],
    )


def fits_planes(mesh):
    return dict(mesh.shape) == {"dp": 2, "blk": 8, "head": 2}


def solution(mesh):
    if fits_planes(mesh):
        body = on_plane
        mesh = jax.sharding.Mesh(mesh.devices.reshape(2, 4, 2, 2), EVERY)
        blk = ("z", "y")
    else:
        body = on_device
        blk = ("blk",)
    token_spec = P("dp", (*blk, "head"), None)
    weight_spec = P(("dp", *blk), "head")
    vector_spec = P(None, ("dp", *blk))
    hidden_spec = P(("dp", *blk))
    return jax.shard_map(
        body,
        mesh=mesh,
        in_specs=(
            token_spec,
            *[weight_spec] * 4,
            vector_spec,
            vector_spec,
            hidden_spec,
            P("dp"),
            token_spec,
        ),
        out_specs=(
            token_spec,
            token_spec,
            *[weight_spec] * 4,
            vector_spec,
            vector_spec,
            hidden_spec,
        ),
        check_vma=False,
    )
```

```python
import jax
import jax.numpy as jnp
from jax import lax
from jax.experimental import pallas as pl
from jax.experimental.pallas import tpu as pltpu
from jax.sharding import PartitionSpec as P

HEADS = 16
HD = 64


EPSILON = 1e-06
NEGATIVE = -1e30


def norm_rows(hidden, gain_vec, shift_vec):
    row_mean = jnp.mean(hidden, axis=-1, keepdims=True)
    centred = hidden - row_mean
    spread = jnp.mean(centred * centred, axis=-1, keepdims=True)
    return centred * lax.rsqrt(spread + EPSILON) * gain_vec + shift_vec


def exact_gelu(values_in):
    return jax.nn.gelu(values_in, approximate=False)


def heads_of(array):
    return array.reshape(array.shape[0], -1, HD)


def masked_scores(query_block, key_block, key_mask, score_scale):
    raw_scores = (
        jnp.einsum("qhd,khd->hqk", query_block, key_block, preferred_element_type=jnp.float32)
        * score_scale
    )
    return jnp.where(key_mask[None, None, :], raw_scores, NEGATIVE)


def full_rows(query_block, key_block, key_mask, score_scale):
    scores = masked_scores(query_block, key_block, key_mask, score_scale)
    row_max = jnp.max(scores, axis=-1, keepdims=True)
    exp_scores = jnp.exp(scores - row_max)
    row_total = jnp.sum(exp_scores, axis=-1, keepdims=True)
    return (exp_scores / row_total, row_max, row_total)


def row_grads(query_block, key_block, value_block, grad_out, key_mask, score_scale):
    softmax_probs, row_max, row_total = full_rows(query_block, key_block, key_mask, score_scale)
    grad_probs = jnp.einsum(
        "qhd,khd->hqk", grad_out, value_block, preferred_element_type=jnp.float32
    )
    row_delta = jnp.sum(softmax_probs * grad_probs, axis=-1, keepdims=True)
    grad_scores = (softmax_probs * (grad_probs - row_delta)).astype(jnp.bfloat16)
    grad_query = (
        jnp.einsum("hqk,khd->qhd", grad_scores, key_block, preferred_element_type=jnp.float32)
        * score_scale
    )
    return (softmax_probs, grad_scores, grad_query, row_max + jnp.log(row_total), row_delta)


def on_device(tokens, w_qkv, w_out, w_up, w_down, gains, biases, up_bias, lengths, cotangent):
    sequences, local_len, width = tokens.shape
    groups = lax.axis_size("head")
    block_len = local_len * groups
    full_len = block_len * lax.axis_size("blk")
    lane_width = HEADS // groups * HD
    score_scale = HD ** (-0.5)
    part_qkv, part_out, part_up, part_down, gain_rows, bias_rows, up_shift = (
        lax.all_gather(w_qkv, ("dp", "blk"), axis=0, tiled=True),
        lax.all_gather(w_out, ("dp", "blk"), axis=0, tiled=True),
        lax.all_gather(w_up, ("dp", "blk"), axis=0, tiled=True),
        lax.all_gather(w_down, ("dp", "blk"), axis=0, tiled=True),
        lax.all_gather(gains, ("dp", "blk"), axis=1, tiled=True),
        lax.all_gather(biases, ("dp", "blk"), axis=1, tiled=True),
        lax.all_gather(up_bias, ("dp", "blk"), axis=0, tiled=True),
    )
    full_qkv, full_out, full_up, full_down = (
        lax.all_gather(part_qkv, "head", axis=1, tiled=True),
        lax.all_gather(part_out, "head", axis=1, tiled=True),
        lax.all_gather(part_up, "head", axis=1, tiled=True),
        lax.all_gather(part_down, "head", axis=1, tiled=True),
    )
    gain_float = gain_rows.astype(jnp.float32)
    bias_float = bias_rows.astype(jnp.float32)
    up_float = up_shift.astype(jnp.float32)
    token_rows = tokens.reshape(sequences * local_len, width)
    qkv_shift = jnp.concatenate([bias_float[0], jnp.zeros((width,), jnp.float32), bias_float[1]])
    projected_all = (
        jnp.dot(token_rows, full_qkv, preferred_element_type=jnp.float32) + qkv_shift
    ).astype(jnp.bfloat16)
    grouped = lax.all_to_all(
        projected_all.reshape(sequences, local_len, 3, groups, lane_width),
        "head",
        split_axis=3,
        concat_axis=1,
        tiled=True,
    )
    queries = grouped[:, :, 0, 0, :]
    key_pairs = grouped[:, :, 1:, 0, :]
    every_pair = lax.all_gather(key_pairs, "blk", axis=1, tiled=True)
    positions = jnp.arange(full_len, dtype=jnp.int32)
    key_valid = positions[None, :] < lengths[:, None]

    def attend(inputs):
        query_block, pair_block, key_mask = inputs
        softmax_probs, row_max, row_total = full_rows(
            heads_of(query_block), heads_of(pair_block[:, 0]), key_mask, score_scale
        )
        attended = jnp.einsum(
            "hqk,khd->qhd",
            softmax_probs.astype(jnp.bfloat16),
            heads_of(pair_block[:, 1]),
            preferred_element_type=jnp.float32,
        )
        return attended.reshape(-1, lane_width).astype(jnp.bfloat16)

    attended_all = lax.map(attend, (queries, every_pair, key_valid))
    returned = lax.all_to_all(
        attended_all[:, :, None, :], "head", split_axis=1, concat_axis=2, tiled=True
    )
    attn_rows = returned.reshape(sequences * local_len, width)
    projected = jnp.dot(attn_rows, full_out, preferred_element_type=jnp.float32) + bias_float[2]
    first_sum = token_rows.astype(jnp.float32) + projected
    normed, first_back = jax.vjp(norm_rows, first_sum, gain_float[0], bias_float[3])
    normed_low = normed.astype(jnp.bfloat16)
    pre_act = jnp.dot(normed_low, full_up, preferred_element_type=jnp.float32) + up_float
    activated, gelu_back = jax.vjp(exact_gelu, pre_act)
    activ_low = activated.astype(jnp.bfloat16)
    second_sum = (
        normed + jnp.dot(activ_low, full_down, preferred_element_type=jnp.float32) + bias_float[4]
    )
    result, second_back = jax.vjp(norm_rows, second_sum, gain_float[1], bias_float[5])
    output = result.astype(jnp.bfloat16).reshape(tokens.shape)
    grad_second, gain_grad_two, shift_grad_two = second_back(
        cotangent.reshape(-1, width).astype(jnp.float32)
    )
    grad_ffn = grad_second.astype(jnp.bfloat16)
    grad_down = jnp.dot(activ_low.T, grad_ffn, preferred_element_type=jnp.float32)
    shift_grad_down = jnp.sum(grad_ffn.astype(jnp.float32), axis=0)
    (grad_act,) = gelu_back(jnp.dot(grad_ffn, full_down.T, preferred_element_type=jnp.float32))
    grad_pre = grad_act.astype(jnp.bfloat16)
    grad_up = jnp.dot(normed_low.T, grad_pre, preferred_element_type=jnp.float32)
    grad_up_shift = jnp.sum(grad_pre.astype(jnp.float32), axis=0)
    grad_normed = grad_second + jnp.dot(grad_pre, full_up.T, preferred_element_type=jnp.float32)
    grad_first, gain_grad_one, shift_grad_one = first_back(grad_normed)
    grad_proj = grad_first.astype(jnp.bfloat16)
    grad_outw = jnp.dot(attn_rows.T, grad_proj, preferred_element_type=jnp.float32)
    shift_grad_out = jnp.sum(grad_proj.astype(jnp.float32), axis=0)
    grad_attn = jnp.dot(grad_proj, full_out.T, preferred_element_type=jnp.float32).astype(
        jnp.bfloat16
    )
    grad_grouped = lax.all_to_all(
        grad_attn.reshape(sequences, local_len, groups, lane_width),
        "head",
        split_axis=2,
        concat_axis=1,
        tiled=True,
    )
    grad_heads = grad_grouped[:, :, 0, :]

    def local_grads(inputs):
        query_block, pair_block, grad_block, key_mask = inputs
        query_heads = heads_of(query_block)
        grad_out = heads_of(grad_block)
        softmax_probs, grad_scores, grad_query, log_total, row_delta = row_grads(
            query_heads,
            heads_of(pair_block[:, 0]),
            heads_of(pair_block[:, 1]),
            grad_out,
            key_mask,
            score_scale,
        )
        grad_keys = (
            jnp.einsum("hqk,qhd->khd", grad_scores, query_heads, preferred_element_type=jnp.float32)
            * score_scale
        )
        grad_values = jnp.einsum(
            "hqk,qhd->khd",
            softmax_probs.astype(jnp.bfloat16),
            grad_out,
            preferred_element_type=jnp.float32,
        )
        key_terms = jnp.stack(
            [grad_keys.reshape(-1, lane_width), grad_values.reshape(-1, lane_width)], axis=1
        )
        return (grad_query.reshape(-1, lane_width).astype(jnp.bfloat16), key_terms)

    grad_queries, key_terms_all = lax.map(local_grads, (queries, every_pair, grad_heads, key_valid))
    grad_pairs = lax.psum_scatter(key_terms_all, "blk", scatter_dimension=1, tiled=True).astype(
        jnp.bfloat16
    )
    grad_mixed = jnp.concatenate([grad_queries[:, :, None, :], grad_pairs], axis=2)
    grad_back = lax.all_to_all(
        grad_mixed[:, :, :, None, :], "head", split_axis=1, concat_axis=3, tiled=True
    )
    grad_rows = grad_back.reshape(sequences * local_len, 3 * width)
    grad_qkv = jnp.dot(token_rows.T, grad_rows, preferred_element_type=jnp.float32)
    column_sums = jnp.sum(grad_rows.astype(jnp.float32), axis=0)
    grad_tokens = (
        grad_first + jnp.dot(grad_rows, full_qkv.T, preferred_element_type=jnp.float32)
    ).reshape(tokens.shape)
    gain_grads = jnp.stack([gain_grad_one, gain_grad_two])
    shift_grads = jnp.stack(
        [
            column_sums[:width],
            column_sums[2 * width :],
            shift_grad_out,
            shift_grad_one,
            shift_grad_down,
            shift_grad_two,
        ]
    )
    cols_qkv, cols_out, cols_up, cols_down = (
        lax.psum_scatter(grad_qkv, "head", scatter_dimension=1, tiled=True),
        lax.psum_scatter(grad_outw, "head", scatter_dimension=1, tiled=True),
        lax.psum_scatter(grad_up, "head", scatter_dimension=1, tiled=True),
        lax.psum_scatter(grad_down, "head", scatter_dimension=1, tiled=True),
    )
    share_qkv, share_out, share_up, share_down, share_gains, share_shifts, share_up_shift = (
        lax.psum_scatter(cols_qkv, ("dp", "blk"), scatter_dimension=0, tiled=True),
        lax.psum_scatter(cols_out, ("dp", "blk"), scatter_dimension=0, tiled=True),
        lax.psum_scatter(cols_up, ("dp", "blk"), scatter_dimension=0, tiled=True),
        lax.psum_scatter(cols_down, ("dp", "blk"), scatter_dimension=0, tiled=True),
        lax.psum_scatter(gain_grads, ("dp", "blk"), scatter_dimension=1, tiled=True),
        lax.psum_scatter(shift_grads, ("dp", "blk"), scatter_dimension=1, tiled=True),
        lax.psum_scatter(grad_up_shift, ("dp", "blk"), scatter_dimension=0, tiled=True),
    )
    total_gains, total_shifts, total_up_shift = lax.psum(
        (share_gains, share_shifts, share_up_shift), "head"
    )
    return (
        output,
        grad_tokens,
        share_qkv,
        share_out,
        share_up,
        share_down,
        total_gains,
        total_shifts,
        total_up_shift,
    )


SWAP = [(0, 1), (1, 0)]
PLANE = ("dp", "y", "head")
LINE = ("dp", "z")
OWNERS = ("dp", "z", "y")
EVERY = ("dp", "z", "y", "head")


def line_pairs(turn):
    return [
        (core * 4 + z, (z // 2) * 4 + 2 * core + (z + turn) % 2)
        for core in range(2)
        for z in range(4)
    ]


def to_planes(array, z_odd):
    first = jnp.where(z_odd, array[1], array[0])
    second = jnp.where(z_odd, array[0], array[1])
    return jnp.concatenate(
        [
            lax.ppermute(first, LINE, line_pairs(0)),
            lax.ppermute(second, LINE, line_pairs(1)),
        ]
    )


def from_planes(rows, z_odd):
    half = rows.shape[0] // 2
    first = lax.ppermute(rows[:half], LINE, [(to, src) for src, to in line_pairs(0)])
    second = lax.ppermute(rows[half:], LINE, [(to, src) for src, to in line_pairs(1)])
    return jnp.stack([jnp.where(z_odd, second, first), jnp.where(z_odd, first, second)])


def swap_x(array):
    return lax.ppermute(array, "head", SWAP)


def swap_y(array):
    return lax.ppermute(array, "y", SWAP)


def swap_xy(array):
    return lax.ppermute(array, ("y", "head"), [(i, 3 - i) for i in range(4)])


def swap_core(array):
    return lax.ppermute(array, "dp", SWAP)


def plane_gather(rows):
    return jnp.concatenate([rows, swap_x(rows), swap_y(rows), swap_xy(rows)])


def plane_sum(terms):
    own, for_x, for_y, for_xy = jnp.split(terms, 4)
    low = jnp.bfloat16
    return (
        own
        + swap_x(for_x.astype(low)).astype(jnp.float32)
        + swap_y(for_y.astype(low)).astype(jnp.float32)
        + swap_xy(for_xy.astype(low)).astype(jnp.float32)
    )


def in_order(flag, own, other):
    return jnp.stack([jnp.where(flag, other, own), jnp.where(flag, own, other)])


def after(value, *others):
    zero = 0.0
    for other in others:
        first = other[(0,) * other.ndim].astype(jnp.float32)
        zero = zero + jnp.minimum(jnp.abs(first), 0.0)
    return value + zero.astype(value.dtype)


NT = (((1,), (1,)), ((), ()))
TN = (((0,), (0,)), ((), ()))
NN = (((1,), (0,)), ((), ()))
WINDOW = 2


def head_part(ref, rows, part, head):
    return ref[rows, part * 2 * HD + head * HD : part * 2 * HD + (head + 1) * HD]


def dotted(left, right, dims):
    return lax.dot_general(left, right, dims, preferred_element_type=jnp.float32)


def column_softmax(keys, scaled, bias):
    scores = dotted(keys, scaled, NT) + bias
    exp_scores = jnp.exp(scores - jnp.max(scores, axis=0, keepdims=True))
    return exp_scores * (1.0 / jnp.sum(exp_scores, axis=0, keepdims=True))


def attend_kernel(slot_ref, qkv_ref, bias_ref, out_ref):
    slot_rows = out_ref.shape[1]
    step = WINDOW * slot_rows
    every = slice(None)
    for block in range(qkv_ref.shape[0] // step):
        found = []
        for head in range(2):
            queries = head_part(qkv_ref, slice(block * step, (block + 1) * step), 0, head)
            scaled = queries * jnp.bfloat16(HD**-0.5)
            probs = column_softmax(head_part(qkv_ref, every, 1, head), scaled, bias_ref[...])
            values = head_part(qkv_ref, every, 2, head)
            found.append(dotted(values, probs.astype(jnp.bfloat16), TN))
        rows = jnp.concatenate(found, axis=0).T.astype(jnp.bfloat16)
        for turn in range(WINDOW):
            place = slot_ref[block * WINDOW + turn]
            out_ref[place] = rows[turn * slot_rows : (turn + 1) * slot_rows]


def attend_back_kernel(slot_ref, qkv_ref, grad_ref, bias_ref, out_ref, probs_ref, scores_ref):
    slot_rows = grad_ref.shape[1]
    step = WINDOW * slot_rows
    every = slice(None)
    low = jnp.bfloat16
    blocks = qkv_ref.shape[0] // step
    grads = jnp.concatenate([grad_ref[slot_ref[i]] for i in range(blocks * WINDOW)], axis=0)
    query_grads, key_grads, value_grads = [], [], []
    for head in range(2):
        keys = head_part(qkv_ref, every, 1, head)
        values = head_part(qkv_ref, every, 2, head)
        scaled = head_part(qkv_ref, every, 0, head) * jnp.bfloat16(HD**-0.5)
        own_grads = grads[:, head * HD : (head + 1) * HD]
        for block in range(blocks):
            part = slice(block * step, (block + 1) * step)
            probs = column_softmax(keys, scaled[part], bias_ref[...])
            grad_probs = dotted(values, own_grads[part], NT)
            delta = jnp.sum(probs * grad_probs, axis=0, keepdims=True)
            probs_ref[:, part] = probs.astype(low)
            scores_ref[:, part] = (probs * (grad_probs - delta)).astype(low)
        query_grads.append(dotted(keys, scores_ref[...], TN) * HD**-0.5)
        key_grads.append(dotted(scores_ref[...], scaled, NN))
        value_grads.append(dotted(probs_ref[...], own_grads, NN))
    out_ref[:, : 2 * HD] = jnp.concatenate(query_grads, axis=0).T.astype(low)
    out_ref[:, 2 * HD : 4 * HD] = jnp.concatenate(key_grads, axis=1).astype(low)
    out_ref[:, 4 * HD :] = jnp.concatenate(value_grads, axis=1).astype(low)


def in_vmem(count):
    return [pl.BlockSpec(memory_space=pltpu.VMEM)] * count


def attend_heads(slots, qkv, bias):
    size = qkv.shape[0]
    return pl.pallas_call(
        attend_kernel,
        out_shape=jax.ShapeDtypeStruct((8, size // 8, 2 * HD), jnp.bfloat16),
        in_specs=[pl.BlockSpec(memory_space=pltpu.SMEM)] + in_vmem(2),
        out_specs=in_vmem(1)[0],
        compiler_params=pltpu.CompilerParams(vmem_limit_bytes=24 * 2**20),
        cost_estimate=pl.CostEstimate(
            flops=8 * size * size * HD, bytes_accessed=8 * size * HD * 2, transcendentals=2 * size**2
        ),
        name="attend",
    )(slots, qkv, bias)


def attend_back(slots, qkv, grads, bias):
    size = qkv.shape[0]
    return pl.pallas_call(
        attend_back_kernel,
        out_shape=jax.ShapeDtypeStruct(qkv.shape, jnp.bfloat16),
        in_specs=[pl.BlockSpec(memory_space=pltpu.SMEM)] + in_vmem(3),
        out_specs=in_vmem(1)[0],
        scratch_shapes=[pltpu.VMEM((size, size), jnp.bfloat16)] * 2,
        compiler_params=pltpu.CompilerParams(vmem_limit_bytes=32 * 2**20),
        cost_estimate=pl.CostEstimate(
            flops=20 * size * size * HD,
            bytes_accessed=14 * size * HD * 2,
            transcendentals=2 * size**2,
        ),
        name="attend_back",
    )(slots, qkv, grads, bias)


def rotated(array, distance):
    return lax.ppermute(array, "z", [(i, (i + distance) % 4) for i in range(4)])


def z_sum(parts, z, axis):
    total = lax.dynamic_index_in_dim(parts, z, axis, keepdims=False)
    for distance in (1, 2, 3):
        sent = lax.dynamic_index_in_dim(parts, (z + distance) % 4, axis, keepdims=False)
        total = total + rotated(sent.astype(jnp.bfloat16), distance).astype(jnp.float32)
    return total


def core_sum(parts, core):
    own = lax.dynamic_index_in_dim(parts, core, 0, keepdims=False)
    sent = lax.dynamic_index_in_dim(parts, 1 - core, 0, keepdims=False)
    return own + swap_core(sent.astype(jnp.bfloat16)).astype(jnp.float32)


def halves_dot(rows, halves):
    return jnp.concatenate(
        [jnp.dot(rows, half, preferred_element_type=jnp.float32) for half in halves], axis=1
    )


def halves_dot_back(rows, halves):
    width = halves.shape[2]
    return jnp.dot(
        rows[:, :width], halves[0].T, preferred_element_type=jnp.float32
    ) + jnp.dot(rows[:, width:], halves[1].T, preferred_element_type=jnp.float32)


def on_plane(tokens, w_qkv, w_out, w_up, w_down, gains, biases, up_bias, lengths, cotangent):
    sequences, local_len, width = tokens.shape
    rows = sequences * local_len
    low, full = jnp.bfloat16, jnp.float32
    core, z, y, x = (lax.axis_index(name) for name in EVERY)
    z_odd = z % 2 == 1
    score_scale = HD ** (-0.5)
    piece = HEADS * HD // 8
    own_d = w_qkv.shape[0]
    hidden_part = up_bias.shape[0]

    token_rows = to_planes(tokens, z_odd)

    groups = w_qkv.reshape(own_d, 3, 4 * piece)
    came = swap_x(groups[:, 1])
    mine = jnp.stack(
        [
            jnp.where(x == 0, groups[:, 0], came),
            jnp.where(x == 0, groups[:, 2], groups[:, 0]),
            jnp.where(x == 0, came, groups[:, 2]),
        ],
        axis=1,
    ).reshape(own_d, 3, 2, 2, piece)
    coded = jnp.concatenate([lengths // 128, lengths % 128]).astype(low)
    small = jnp.concatenate([gains.reshape(-1), biases.reshape(-1), up_bias, coded])
    extra = jnp.pad(small, (0, 8 * 3 * piece - small.shape[0])).reshape(8, 3 * piece)
    shares = jnp.concatenate(
        [
            mine.transpose(2, 3, 0, 1, 4).reshape(2, 2, own_d, 3 * piece),
            jnp.broadcast_to(extra, (2, 2, 8, 3 * piece)),
        ],
        axis=2,
    )
    y_kept = lax.dynamic_index_in_dim(shares, y, 0, keepdims=False)
    y_given = lax.dynamic_index_in_dim(shares, 1 - y, 0, keepdims=False)
    shares = in_order(y == 1, y_kept, swap_y(y_given))
    core_kept = lax.dynamic_index_in_dim(shares, core, 1, keepdims=False)
    core_given = lax.dynamic_index_in_dim(shares, 1 - core, 1, keepdims=False)
    shares = in_order(core == 1, core_kept, swap_core(core_given))
    gathered = jnp.zeros((2, 4, 2, own_d + 8, 3 * piece), low)
    gathered = lax.dynamic_update_index_in_dim(gathered, shares, z, 1)
    for distance in (1, 2, 3):
        gathered = lax.dynamic_update_index_in_dim(
            gathered, rotated(shares, distance), (z - distance) % 4, 1
        )
    dev_qkv = gathered[:, :, :, :own_d].reshape(width, 3 * piece)
    small_all = gathered[:, :, :, own_d:].reshape(16, 8 * 3 * piece).astype(full)
    vectors = small_all[:, : 8 * own_d].reshape(16, 8, own_d).transpose(1, 0, 2).reshape(8, width)
    gain_float, bias_float = vectors[:2], vectors[2:]
    up_parts = small_all[:, 8 * own_d : 8 * own_d + hidden_part].reshape(2, 4, 2, hidden_part)
    up_float = lax.dynamic_index_in_dim(
        lax.dynamic_index_in_dim(up_parts, x, 0, keepdims=False), y, 1, keepdims=False
    ).reshape(4 * hidden_part)
    code = small_all[z // 2 * 8, 8 * own_d + hidden_part :][:4]
    length = (code[z % 2] * 128 + code[2 + z % 2]).astype(jnp.int32)

    out_halves = lax.all_gather(w_out, ("head", *OWNERS)).reshape(2, width, width // 2)

    up_split = w_up.reshape(own_d, 4, 2, hidden_part)
    up_kept = lax.dynamic_index_in_dim(up_split, y, 2, keepdims=False)
    up_given = lax.dynamic_index_in_dim(up_split, 1 - y, 2, keepdims=False)
    up_rows = in_order(y == 1, up_kept, swap_y(up_given)).reshape(2 * own_d, 4 * hidden_part)
    up_rows = after(up_rows, out_halves)
    dev_up = lax.all_gather(up_rows, LINE, axis=0, tiled=True)

    corner = [(0, 0), (1, 2), (2, 1), (3, 3)]
    down_rows = lax.ppermute(w_down, ("dp", "head"), corner)
    down_rows = after(down_rows, dev_up)
    down_halves = lax.all_gather(down_rows, LINE).reshape(2, 4 * hidden_part, width // 2)

    cotangent_rows = to_planes(cotangent, z_odd)

    core_rows = plane_gather(token_rows)
    all_rows = jnp.concatenate([core_rows, swap_core(core_rows)])

    first_col = (x * 8 + y * 4 + core * 2) * HD
    query_shift = lax.dynamic_slice_in_dim(bias_float[0], first_col, piece)
    value_shift = lax.dynamic_slice_in_dim(bias_float[1], first_col, piece)
    qkv_shift = jnp.concatenate([query_shift, jnp.zeros((piece,), full), value_shift])
    qkv = (jnp.dot(all_rows, dev_qkv, preferred_element_type=full) + qkv_shift).astype(low)
    slot = jnp.arange(8, dtype=jnp.int32)
    slots = slot ^ (core * 4 + y * 2 + x)
    slot_core, slot_y, slot_x = slots // 4, slots // 2 % 2, slots % 2
    turn = jnp.arange(2, dtype=jnp.int32)
    from_z = 2 * slot_core[:, None] + (z + turn[None, :]) % 2
    block = (from_z * 2 + slot_y[:, None]) * 2 + slot_x[:, None]
    positions = block[:, :, None] * local_len + jnp.arange(local_len, dtype=jnp.int32)
    bias = jnp.where(positions.reshape(-1, 1) < length, 0.0, NEGATIVE).astype(full)
    attended = attend_heads(slots, qkv, bias)
    returned = lax.all_to_all(attended, PLANE, split_axis=0, concat_axis=0, tiled=True)
    attn_rows = (
        returned.reshape(2, 2, 2, rows, piece).transpose(3, 2, 1, 0, 4).reshape(rows, width)
    )
    projected = halves_dot(attn_rows, out_halves) + bias_float[2]
    first_sum = token_rows.astype(full) + projected
    normed, first_back = jax.vjp(norm_rows, first_sum, gain_float[0], bias_float[3])

    swaps = (swap_x, swap_y, swap_xy)
    normed_low = normed.astype(low)
    normed_parts = [normed_low] + [swap(normed_low) for swap in swaps]
    activ_parts, gelu_backs, ffn_terms = [], [], []
    for part in normed_parts:
        pre_act = jnp.dot(part, dev_up, preferred_element_type=full) + up_float
        activated, gelu_back = jax.vjp(exact_gelu, pre_act)
        activ_parts.append(activated.astype(low))
        gelu_backs.append(gelu_back)
        ffn_terms.append(halves_dot(activ_parts[-1], down_halves))
    ffn_out = ffn_terms[0]
    for swap, term in zip(swaps, ffn_terms[1:]):
        ffn_out = ffn_out + swap(term.astype(low)).astype(full)
    second_sum = normed + ffn_out + bias_float[4]
    result, second_back = jax.vjp(norm_rows, second_sum, gain_float[1], bias_float[5])
    output = from_planes(result.astype(low), z_odd)
    grad_second, gain_grad_two, shift_grad_two = second_back(cotangent_rows.astype(full))
    grad_ffn = grad_second.astype(low)
    shift_grad_down = jnp.sum(grad_ffn.astype(full), axis=0)

    ffn_parts = [grad_ffn] + [swap(grad_ffn) for swap in swaps]
    pre_parts, back_terms = [], []
    for part, gelu_back in zip(ffn_parts, gelu_backs):
        (grad_act,) = gelu_back(halves_dot_back(part, down_halves))
        pre_parts.append(grad_act.astype(low))
        back_terms.append(jnp.dot(pre_parts[-1], dev_up.T, preferred_element_type=full))
    back_sent = [swap(term.astype(low)) for swap, term in zip(swaps, back_terms[1:])]

    ffn_all = jnp.concatenate(ffn_parts)
    activ_all = jnp.concatenate(activ_parts)
    grad_down = jnp.einsum(
        "th,tcd->chd",
        activ_all,
        ffn_all.reshape(4 * rows, 2, width // 2),
        preferred_element_type=full,
    )
    grad_down = core_sum(grad_down, core)
    grad_normed = grad_second + back_terms[0]
    for sent in back_sent:
        grad_normed = grad_normed + sent.astype(full)
    down_total = z_sum(grad_down.reshape(4, hidden_part, width // 2), z, 0)
    share_down = lax.ppermute(down_total.astype(low), ("dp", "head"), corner).astype(full)

    pre_all = jnp.concatenate(pre_parts)
    normed_all = jnp.concatenate(normed_parts)
    grad_up_shift = jnp.sum(pre_all.astype(full), axis=0)
    grad_up = jnp.dot(normed_all.T, pre_all, preferred_element_type=full)
    grad_up = core_sum(grad_up.reshape(2, 8 * own_d, 4 * hidden_part), core)

    grad_first, gain_grad_one, shift_grad_one = first_back(grad_normed)
    grad_proj = grad_first.astype(low)
    shift_grad_out = jnp.sum(grad_proj.astype(full), axis=0)
    grad_attn = halves_dot_back(grad_proj, out_halves).astype(low)
    grad_out = lax.all_to_all(
        grad_attn.reshape(rows, 2, 2, 2, piece).transpose(3, 2, 1, 0, 4).reshape(8, rows, piece),
        PLANE,
        split_axis=0,
        concat_axis=0,
        tiled=True,
    )
    up_terms = after(grad_up.reshape(4, 2 * own_d, 4 * hidden_part), down_total)
    share_up = z_sum(up_terms, z, 0).astype(low)
    up_total = share_up
    share_up = share_up.reshape(2, own_d, 4, hidden_part)
    up_home = lax.dynamic_index_in_dim(share_up, y, 0, keepdims=False)
    up_away = lax.dynamic_index_in_dim(share_up, 1 - y, 0, keepdims=False)
    share_up = (
        in_order(y == 1, up_home, swap_y(up_away))
        .transpose(1, 2, 0, 3)
        .reshape(own_d, 8 * hidden_part)
        .astype(full)
    )

    grad_outw = jnp.dot(attn_rows.T, grad_proj, preferred_element_type=full)
    grad_outw = core_sum(grad_outw.reshape(2, 4, 2, own_d, width), core)
    out_home = lax.dynamic_index_in_dim(grad_outw, y, 1, keepdims=False)
    out_away = lax.dynamic_index_in_dim(grad_outw, 1 - y, 1, keepdims=False)
    grad_outw = out_home + swap_y(out_away.astype(low)).astype(full)
    grad_outw = grad_outw.reshape(4, own_d, 2, width // 2)
    out_home = lax.dynamic_index_in_dim(grad_outw, x, 2, keepdims=False)
    out_away = lax.dynamic_index_in_dim(grad_outw, 1 - x, 2, keepdims=False)
    grad_outw = out_home + swap_x(out_away.astype(low)).astype(full)
    share_out = z_sum(after(grad_outw, up_total), z, 0)

    vector_grads = jnp.stack(
        [
            gain_grad_one,
            gain_grad_two,
            shift_grad_out,
            shift_grad_one,
            shift_grad_down,
            shift_grad_two,
        ]
    )
    vector_grads = vector_grads.reshape(6, 16, own_d).transpose(1, 0, 2).reshape(16, 6 * own_d)
    at_core = (jnp.arange(2) == x)[:, None, None, None]
    at_y = (jnp.arange(2) == y)[None, None, :, None]
    up_grads = jnp.where(at_core & at_y, grad_up_shift.reshape(1, 4, 1, hidden_part), 0.0)
    small_grads = jnp.concatenate([vector_grads, up_grads.reshape(16, hidden_part)], axis=1)
    small_grads = jnp.repeat(small_grads, 2, axis=0)
    small_back = lax.all_to_all(small_grads, EVERY, split_axis=0, concat_axis=0, tiled=True)
    small_total = jnp.sum(small_back, axis=0)

    grad_qkv = attend_back(slots, qkv, grad_out, bias)
    column_sums = jnp.sum(grad_qkv.astype(full), axis=0)

    back_terms = jnp.dot(grad_qkv, dev_qkv.T, preferred_element_type=full)
    core_terms = back_terms[: 4 * rows] + swap_core(back_terms[4 * rows :].astype(low)).astype(full)
    grad_rows = grad_first + plane_sum(core_terms)
    grad_tokens = from_planes(grad_rows.astype(low), z_odd).astype(full)

    grad_w = jnp.dot(all_rows.T, grad_qkv, preferred_element_type=full)
    grad_w = after(grad_w.reshape(2, 4, 2, own_d, 3 * piece), share_out)
    grad_w = z_sum(grad_w, z, 1).astype(low)
    sent = jnp.stack([grad_w[..., : 2 * piece], grad_w[..., piece:]], axis=2)
    back = lax.all_to_all(
        sent.reshape(8, own_d, 2 * piece), PLANE, split_axis=0, concat_axis=0, tiled=True
    )
    back = back.reshape(2, 2, 2, own_d, 2, piece).transpose(3, 4, 2, 1, 0, 5)
    back = back.reshape(own_d, 2, 2, 4 * piece)
    share_qkv = jnp.concatenate(
        [
            jnp.where(x == 0, back[:, 0, 0], back[:, 0, 1]),
            jnp.where(x == 0, back[:, 0, 1], back[:, 1, 0]),
            jnp.where(x == 0, back[:, 1, 0], back[:, 1, 1]),
        ],
        axis=1,
    ).astype(full)

    late = jnp.stack([column_sums[:piece], column_sums[2 * piece :]]).reshape(2, 2, own_d)
    late = late.transpose(1, 0, 2).reshape(1, 1, 2, 1, 2 * own_d)
    at_z = (jnp.arange(4) == 2 * y + core)[None, :, None, None, None]
    late = jnp.where(at_core[..., None] & at_z, late, 0.0)
    late = jnp.broadcast_to(late, (2, 4, 2, 2, 2 * own_d)).reshape(32, 2 * own_d)
    late_back = lax.all_to_all(late, EVERY, split_axis=0, concat_axis=0, tiled=True)
    late_total = jnp.sum(late_back, axis=0).reshape(2, own_d)
    vector_total = small_total[: 6 * own_d].reshape(6, own_d)
    return (
        output,
        grad_tokens,
        share_qkv,
        share_out,
        share_up,
        share_down,
        vector_total[:2],
        jnp.concatenate([late_total, vector_total[2:]]),
        small_total[6 * own_d :],
    )


def fits_planes(mesh):
    return dict(mesh.shape) == {"dp": 2, "blk": 8, "head": 2}


def solution(mesh):
    if fits_planes(mesh):
        body = on_plane
        mesh = jax.sharding.Mesh(mesh.devices.reshape(2, 4, 2, 2), EVERY)
        blk = ("z", "y")
    else:
        body = on_device
        blk = ("blk",)
    token_spec = P("dp", (*blk, "head"), None)
    weight_spec = P(("dp", *blk), "head")
    vector_spec = P(None, ("dp", *blk))
    hidden_spec = P(("dp", *blk))
    return jax.shard_map(
        body,
        mesh=mesh,
        in_specs=(
            token_spec,
            *[weight_spec] * 4,
            vector_spec,
            vector_spec,
            hidden_spec,
            P("dp"),
            token_spec,
        ),
        out_specs=(
            token_spec,
            token_spec,
            *[weight_spec] * 4,
            vector_spec,
            vector_spec,
            hidden_spec,
        ),
        check_vma=False,
    )
```

```python
import jax
import jax.numpy as jnp
from jax import lax
from jax.experimental import pallas as pl
from jax.experimental.pallas import tpu as pltpu
from jax.sharding import PartitionSpec as P

HEADS = 16
HD = 64


EPSILON = 1e-06
NEGATIVE = -1e30


def norm_rows(hidden, gain_vec, shift_vec):
    row_mean = jnp.mean(hidden, axis=-1, keepdims=True)
    centred = hidden - row_mean
    spread = jnp.mean(centred * centred, axis=-1, keepdims=True)
    return centred * lax.rsqrt(spread + EPSILON) * gain_vec + shift_vec


def exact_gelu(values_in):
    return jax.nn.gelu(values_in, approximate=False)


def heads_of(array):
    return array.reshape(array.shape[0], -1, HD)


def masked_scores(query_block, key_block, key_mask, score_scale):
    raw_scores = (
        jnp.einsum("qhd,khd->hqk", query_block, key_block, preferred_element_type=jnp.float32)
        * score_scale
    )
    return jnp.where(key_mask[None, None, :], raw_scores, NEGATIVE)


def full_rows(query_block, key_block, key_mask, score_scale):
    scores = masked_scores(query_block, key_block, key_mask, score_scale)
    row_max = jnp.max(scores, axis=-1, keepdims=True)
    exp_scores = jnp.exp(scores - row_max)
    row_total = jnp.sum(exp_scores, axis=-1, keepdims=True)
    return (exp_scores / row_total, row_max, row_total)


def row_grads(query_block, key_block, value_block, grad_out, key_mask, score_scale):
    softmax_probs, row_max, row_total = full_rows(query_block, key_block, key_mask, score_scale)
    grad_probs = jnp.einsum(
        "qhd,khd->hqk", grad_out, value_block, preferred_element_type=jnp.float32
    )
    row_delta = jnp.sum(softmax_probs * grad_probs, axis=-1, keepdims=True)
    grad_scores = (softmax_probs * (grad_probs - row_delta)).astype(jnp.bfloat16)
    grad_query = (
        jnp.einsum("hqk,khd->qhd", grad_scores, key_block, preferred_element_type=jnp.float32)
        * score_scale
    )
    return (softmax_probs, grad_scores, grad_query, row_max + jnp.log(row_total), row_delta)


def on_device(tokens, w_qkv, w_out, w_up, w_down, gains, biases, up_bias, lengths, cotangent):
    sequences, local_len, width = tokens.shape
    groups = lax.axis_size("head")
    block_len = local_len * groups
    full_len = block_len * lax.axis_size("blk")
    lane_width = HEADS // groups * HD
    score_scale = HD ** (-0.5)
    part_qkv, part_out, part_up, part_down, gain_rows, bias_rows, up_shift = (
        lax.all_gather(w_qkv, ("dp", "blk"), axis=0, tiled=True),
        lax.all_gather(w_out, ("dp", "blk"), axis=0, tiled=True),
        lax.all_gather(w_up, ("dp", "blk"), axis=0, tiled=True),
        lax.all_gather(w_down, ("dp", "blk"), axis=0, tiled=True),
        lax.all_gather(gains, ("dp", "blk"), axis=1, tiled=True),
        lax.all_gather(biases, ("dp", "blk"), axis=1, tiled=True),
        lax.all_gather(up_bias, ("dp", "blk"), axis=0, tiled=True),
    )
    full_qkv, full_out, full_up, full_down = (
        lax.all_gather(part_qkv, "head", axis=1, tiled=True),
        lax.all_gather(part_out, "head", axis=1, tiled=True),
        lax.all_gather(part_up, "head", axis=1, tiled=True),
        lax.all_gather(part_down, "head", axis=1, tiled=True),
    )
    gain_float = gain_rows.astype(jnp.float32)
    bias_float = bias_rows.astype(jnp.float32)
    up_float = up_shift.astype(jnp.float32)
    token_rows = tokens.reshape(sequences * local_len, width)
    qkv_shift = jnp.concatenate([bias_float[0], jnp.zeros((width,), jnp.float32), bias_float[1]])
    projected_all = (
        jnp.dot(token_rows, full_qkv, preferred_element_type=jnp.float32) + qkv_shift
    ).astype(jnp.bfloat16)
    grouped = lax.all_to_all(
        projected_all.reshape(sequences, local_len, 3, groups, lane_width),
        "head",
        split_axis=3,
        concat_axis=1,
        tiled=True,
    )
    queries = grouped[:, :, 0, 0, :]
    key_pairs = grouped[:, :, 1:, 0, :]
    every_pair = lax.all_gather(key_pairs, "blk", axis=1, tiled=True)
    positions = jnp.arange(full_len, dtype=jnp.int32)
    key_valid = positions[None, :] < lengths[:, None]

    def attend(inputs):
        query_block, pair_block, key_mask = inputs
        softmax_probs, row_max, row_total = full_rows(
            heads_of(query_block), heads_of(pair_block[:, 0]), key_mask, score_scale
        )
        attended = jnp.einsum(
            "hqk,khd->qhd",
            softmax_probs.astype(jnp.bfloat16),
            heads_of(pair_block[:, 1]),
            preferred_element_type=jnp.float32,
        )
        return attended.reshape(-1, lane_width).astype(jnp.bfloat16)

    attended_all = lax.map(attend, (queries, every_pair, key_valid))
    returned = lax.all_to_all(
        attended_all[:, :, None, :], "head", split_axis=1, concat_axis=2, tiled=True
    )
    attn_rows = returned.reshape(sequences * local_len, width)
    projected = jnp.dot(attn_rows, full_out, preferred_element_type=jnp.float32) + bias_float[2]
    first_sum = token_rows.astype(jnp.float32) + projected
    normed, first_back = jax.vjp(norm_rows, first_sum, gain_float[0], bias_float[3])
    normed_low = normed.astype(jnp.bfloat16)
    pre_act = jnp.dot(normed_low, full_up, preferred_element_type=jnp.float32) + up_float
    activated, gelu_back = jax.vjp(exact_gelu, pre_act)
    activ_low = activated.astype(jnp.bfloat16)
    second_sum = (
        normed + jnp.dot(activ_low, full_down, preferred_element_type=jnp.float32) + bias_float[4]
    )
    result, second_back = jax.vjp(norm_rows, second_sum, gain_float[1], bias_float[5])
    output = result.astype(jnp.bfloat16).reshape(tokens.shape)
    grad_second, gain_grad_two, shift_grad_two = second_back(
        cotangent.reshape(-1, width).astype(jnp.float32)
    )
    grad_ffn = grad_second.astype(jnp.bfloat16)
    grad_down = jnp.dot(activ_low.T, grad_ffn, preferred_element_type=jnp.float32)
    shift_grad_down = jnp.sum(grad_ffn.astype(jnp.float32), axis=0)
    (grad_act,) = gelu_back(jnp.dot(grad_ffn, full_down.T, preferred_element_type=jnp.float32))
    grad_pre = grad_act.astype(jnp.bfloat16)
    grad_up = jnp.dot(normed_low.T, grad_pre, preferred_element_type=jnp.float32)
    grad_up_shift = jnp.sum(grad_pre.astype(jnp.float32), axis=0)
    grad_normed = grad_second + jnp.dot(grad_pre, full_up.T, preferred_element_type=jnp.float32)
    grad_first, gain_grad_one, shift_grad_one = first_back(grad_normed)
    grad_proj = grad_first.astype(jnp.bfloat16)
    grad_outw = jnp.dot(attn_rows.T, grad_proj, preferred_element_type=jnp.float32)
    shift_grad_out = jnp.sum(grad_proj.astype(jnp.float32), axis=0)
    grad_attn = jnp.dot(grad_proj, full_out.T, preferred_element_type=jnp.float32).astype(
        jnp.bfloat16
    )
    grad_grouped = lax.all_to_all(
        grad_attn.reshape(sequences, local_len, groups, lane_width),
        "head",
        split_axis=2,
        concat_axis=1,
        tiled=True,
    )
    grad_heads = grad_grouped[:, :, 0, :]

    def local_grads(inputs):
        query_block, pair_block, grad_block, key_mask = inputs
        query_heads = heads_of(query_block)
        grad_out = heads_of(grad_block)
        softmax_probs, grad_scores, grad_query, log_total, row_delta = row_grads(
            query_heads,
            heads_of(pair_block[:, 0]),
            heads_of(pair_block[:, 1]),
            grad_out,
            key_mask,
            score_scale,
        )
        grad_keys = (
            jnp.einsum("hqk,qhd->khd", grad_scores, query_heads, preferred_element_type=jnp.float32)
            * score_scale
        )
        grad_values = jnp.einsum(
            "hqk,qhd->khd",
            softmax_probs.astype(jnp.bfloat16),
            grad_out,
            preferred_element_type=jnp.float32,
        )
        key_terms = jnp.stack(
            [grad_keys.reshape(-1, lane_width), grad_values.reshape(-1, lane_width)], axis=1
        )
        return (grad_query.reshape(-1, lane_width).astype(jnp.bfloat16), key_terms)

    grad_queries, key_terms_all = lax.map(local_grads, (queries, every_pair, grad_heads, key_valid))
    grad_pairs = lax.psum_scatter(key_terms_all, "blk", scatter_dimension=1, tiled=True).astype(
        jnp.bfloat16
    )
    grad_mixed = jnp.concatenate([grad_queries[:, :, None, :], grad_pairs], axis=2)
    grad_back = lax.all_to_all(
        grad_mixed[:, :, :, None, :], "head", split_axis=1, concat_axis=3, tiled=True
    )
    grad_rows = grad_back.reshape(sequences * local_len, 3 * width)
    grad_qkv = jnp.dot(token_rows.T, grad_rows, preferred_element_type=jnp.float32)
    column_sums = jnp.sum(grad_rows.astype(jnp.float32), axis=0)
    grad_tokens = (
        grad_first + jnp.dot(grad_rows, full_qkv.T, preferred_element_type=jnp.float32)
    ).reshape(tokens.shape)
    gain_grads = jnp.stack([gain_grad_one, gain_grad_two])
    shift_grads = jnp.stack(
        [
            column_sums[:width],
            column_sums[2 * width :],
            shift_grad_out,
            shift_grad_one,
            shift_grad_down,
            shift_grad_two,
        ]
    )
    cols_qkv, cols_out, cols_up, cols_down = (
        lax.psum_scatter(grad_qkv, "head", scatter_dimension=1, tiled=True),
        lax.psum_scatter(grad_outw, "head", scatter_dimension=1, tiled=True),
        lax.psum_scatter(grad_up, "head", scatter_dimension=1, tiled=True),
        lax.psum_scatter(grad_down, "head", scatter_dimension=1, tiled=True),
    )
    share_qkv, share_out, share_up, share_down, share_gains, share_shifts, share_up_shift = (
        lax.psum_scatter(cols_qkv, ("dp", "blk"), scatter_dimension=0, tiled=True),
        lax.psum_scatter(cols_out, ("dp", "blk"), scatter_dimension=0, tiled=True),
        lax.psum_scatter(cols_up, ("dp", "blk"), scatter_dimension=0, tiled=True),
        lax.psum_scatter(cols_down, ("dp", "blk"), scatter_dimension=0, tiled=True),
        lax.psum_scatter(gain_grads, ("dp", "blk"), scatter_dimension=1, tiled=True),
        lax.psum_scatter(shift_grads, ("dp", "blk"), scatter_dimension=1, tiled=True),
        lax.psum_scatter(grad_up_shift, ("dp", "blk"), scatter_dimension=0, tiled=True),
    )
    total_gains, total_shifts, total_up_shift = lax.psum(
        (share_gains, share_shifts, share_up_shift), "head"
    )
    return (
        output,
        grad_tokens,
        share_qkv,
        share_out,
        share_up,
        share_down,
        total_gains,
        total_shifts,
        total_up_shift,
    )


SWAP = [(0, 1), (1, 0)]
PLANE = ("dp", "y", "head")
LINE = ("dp", "z")
OWNERS = ("dp", "z", "y")
EVERY = ("dp", "z", "y", "head")


def line_pairs(turn):
    return [
        (core * 4 + z, (z // 2) * 4 + 2 * core + (z + turn) % 2)
        for core in range(2)
        for z in range(4)
    ]


def to_planes(array, z_odd):
    first = jnp.where(z_odd, array[1], array[0])
    second = jnp.where(z_odd, array[0], array[1])
    return jnp.concatenate(
        [
            lax.ppermute(first, LINE, line_pairs(0)),
            lax.ppermute(second, LINE, line_pairs(1)),
        ]
    )


def from_planes(rows, z_odd):
    half = rows.shape[0] // 2
    first = lax.ppermute(rows[:half], LINE, [(to, src) for src, to in line_pairs(0)])
    second = lax.ppermute(rows[half:], LINE, [(to, src) for src, to in line_pairs(1)])
    return jnp.stack([jnp.where(z_odd, second, first), jnp.where(z_odd, first, second)])


def swap_x(array):
    return lax.ppermute(array, "head", SWAP)


def swap_y(array):
    return lax.ppermute(array, "y", SWAP)


def swap_xy(array):
    return lax.ppermute(array, ("y", "head"), [(i, 3 - i) for i in range(4)])


def swap_core(array):
    return lax.ppermute(array, "dp", SWAP)


def plane_gather(rows):
    return jnp.concatenate([rows, swap_x(rows), swap_y(rows), swap_xy(rows)])


def plane_sum(terms):
    own, for_x, for_y, for_xy = jnp.split(terms, 4)
    low = jnp.bfloat16
    return (
        own
        + swap_x(for_x.astype(low)).astype(jnp.float32)
        + swap_y(for_y.astype(low)).astype(jnp.float32)
        + swap_xy(for_xy.astype(low)).astype(jnp.float32)
    )


def in_order(flag, own, other):
    return jnp.stack([jnp.where(flag, other, own), jnp.where(flag, own, other)])


def after(value, *others):
    zero = 0.0
    for other in others:
        first = other[(0,) * other.ndim].astype(jnp.float32)
        zero = zero + jnp.minimum(jnp.abs(first), 0.0)
    return value + zero.astype(value.dtype)


NT = (((1,), (1,)), ((), ()))
TN = (((0,), (0,)), ((), ()))
NN = (((1,), (0,)), ((), ()))
WINDOW = 2


def head_part(ref, rows, part, head):
    return ref[rows, part * 2 * HD + head * HD : part * 2 * HD + (head + 1) * HD]


def dotted(left, right, dims):
    return lax.dot_general(left, right, dims, preferred_element_type=jnp.float32)


def column_softmax(keys, scaled, bias):
    scores = dotted(keys, scaled, NT) + bias
    exp_scores = jnp.exp(scores - jnp.max(scores, axis=0, keepdims=True))
    return exp_scores * (1.0 / jnp.sum(exp_scores, axis=0, keepdims=True))


def attend_kernel(slot_ref, qkv_ref, bias_ref, out_ref):
    slot_rows = out_ref.shape[1]
    step = WINDOW * slot_rows
    every = slice(None)
    for block in range(qkv_ref.shape[0] // step):
        found = []
        for head in range(2):
            queries = head_part(qkv_ref, slice(block * step, (block + 1) * step), 0, head)
            scaled = queries * jnp.bfloat16(HD**-0.5)
            probs = column_softmax(head_part(qkv_ref, every, 1, head), scaled, bias_ref[...])
            values = head_part(qkv_ref, every, 2, head)
            found.append(dotted(values, probs.astype(jnp.bfloat16), TN))
        rows = jnp.concatenate(found, axis=0).T.astype(jnp.bfloat16)
        for turn in range(WINDOW):
            place = slot_ref[block * WINDOW + turn]
            out_ref[place] = rows[turn * slot_rows : (turn + 1) * slot_rows]


def attend_back_kernel(slot_ref, qkv_ref, grad_ref, bias_ref, out_ref, probs_ref, scores_ref):
    slot_rows = grad_ref.shape[1]
    step = WINDOW * slot_rows
    every = slice(None)
    low = jnp.bfloat16
    blocks = qkv_ref.shape[0] // step
    grads = jnp.concatenate([grad_ref[slot_ref[i]] for i in range(blocks * WINDOW)], axis=0)
    query_grads, key_grads, value_grads = [], [], []
    for head in range(2):
        keys = head_part(qkv_ref, every, 1, head)
        values = head_part(qkv_ref, every, 2, head)
        scaled = head_part(qkv_ref, every, 0, head) * jnp.bfloat16(HD**-0.5)
        own_grads = grads[:, head * HD : (head + 1) * HD]
        for block in range(blocks):
            part = slice(block * step, (block + 1) * step)
            probs = column_softmax(keys, scaled[part], bias_ref[...])
            grad_probs = dotted(values, own_grads[part], NT)
            delta = jnp.sum(probs * grad_probs, axis=0, keepdims=True)
            probs_ref[:, part] = probs.astype(low)
            scores_ref[:, part] = (probs * (grad_probs - delta)).astype(low)
        query_grads.append(dotted(keys, scores_ref[...], TN) * HD**-0.5)
        key_grads.append(dotted(scores_ref[...], scaled, NN))
        value_grads.append(dotted(probs_ref[...], own_grads, NN))
    out_ref[:, : 2 * HD] = jnp.concatenate(query_grads, axis=0).T.astype(low)
    out_ref[:, 2 * HD : 4 * HD] = jnp.concatenate(key_grads, axis=1).astype(low)
    out_ref[:, 4 * HD :] = jnp.concatenate(value_grads, axis=1).astype(low)


def in_vmem(count):
    return [pl.BlockSpec(memory_space=pltpu.VMEM)] * count


def attend_heads(slots, qkv, bias):
    size = qkv.shape[0]
    return pl.pallas_call(
        attend_kernel,
        out_shape=jax.ShapeDtypeStruct((8, size // 8, 2 * HD), jnp.bfloat16),
        in_specs=[pl.BlockSpec(memory_space=pltpu.SMEM)] + in_vmem(2),
        out_specs=in_vmem(1)[0],
        compiler_params=pltpu.CompilerParams(vmem_limit_bytes=24 * 2**20),
        cost_estimate=pl.CostEstimate(
            flops=128 * size * size * HD,
            bytes_accessed=8 * size * HD * 2,
            transcendentals=2 * size**2,
        ),
        name="attend",
    )(slots, qkv, bias)


def attend_back(slots, qkv, grads, bias):
    size = qkv.shape[0]
    return pl.pallas_call(
        attend_back_kernel,
        out_shape=jax.ShapeDtypeStruct(qkv.shape, jnp.bfloat16),
        in_specs=[pl.BlockSpec(memory_space=pltpu.SMEM)] + in_vmem(3),
        out_specs=in_vmem(1)[0],
        scratch_shapes=[pltpu.VMEM((size, size), jnp.bfloat16)] * 2,
        compiler_params=pltpu.CompilerParams(vmem_limit_bytes=32 * 2**20),
        cost_estimate=pl.CostEstimate(
            flops=140 * size * size * HD,
            bytes_accessed=14 * size * HD * 2,
            transcendentals=2 * size**2,
        ),
        name="attend_back",
    )(slots, qkv, grads, bias)


def exchanged(parts, axes):
    return lax.all_to_all(parts, axes, split_axis=0, concat_axis=0, tiled=True)


def spread(array, axes):
    return exchanged(jnp.broadcast_to(array, (4, *array.shape)), axes)


def term_sum(parts, axes):
    return jnp.sum(exchanged(parts.astype(jnp.bfloat16), axes).astype(jnp.float32), axis=0)


def core_sum(parts, core):
    own = lax.dynamic_index_in_dim(parts, core, 0, keepdims=False)
    sent = lax.dynamic_index_in_dim(parts, 1 - core, 0, keepdims=False)
    return own + swap_core(sent.astype(jnp.bfloat16)).astype(jnp.float32)


def halves_dot(rows, halves):
    return jnp.concatenate(
        [jnp.dot(rows, half, preferred_element_type=jnp.float32) for half in halves], axis=1
    )


def halves_dot_back(rows, halves):
    width = halves.shape[2]
    return jnp.dot(
        rows[:, :width], halves[0].T, preferred_element_type=jnp.float32
    ) + jnp.dot(rows[:, width:], halves[1].T, preferred_element_type=jnp.float32)


def on_plane(tokens, w_qkv, w_out, w_up, w_down, gains, biases, up_bias, lengths, cotangent):
    sequences, local_len, width = tokens.shape
    rows = sequences * local_len
    low, full = jnp.bfloat16, jnp.float32
    core, z, y, x = (lax.axis_index(name) for name in EVERY)
    z_odd = z % 2 == 1
    score_scale = HD ** (-0.5)
    piece = HEADS * HD // 8
    own_d = w_qkv.shape[0]
    hidden_part = up_bias.shape[0]

    token_rows = to_planes(tokens, z_odd)

    groups = w_qkv.reshape(own_d, 3, 4 * piece)
    came = swap_x(groups[:, 1])
    mine = jnp.stack(
        [
            jnp.where(x == 0, groups[:, 0], came),
            jnp.where(x == 0, groups[:, 2], groups[:, 0]),
            jnp.where(x == 0, came, groups[:, 2]),
        ],
        axis=1,
    ).reshape(own_d, 3, 2, 2, piece)
    coded = jnp.concatenate([lengths // 128, lengths % 128]).astype(low)
    small = jnp.concatenate([gains.reshape(-1), biases.reshape(-1), up_bias, coded])
    extra = jnp.pad(small, (0, 8 * 3 * piece - small.shape[0])).reshape(8, 3 * piece)
    shares = jnp.concatenate(
        [
            mine.transpose(2, 3, 0, 1, 4).reshape(2, 2, own_d, 3 * piece),
            jnp.broadcast_to(extra, (2, 2, 8, 3 * piece)),
        ],
        axis=2,
    )
    y_kept = lax.dynamic_index_in_dim(shares, y, 0, keepdims=False)
    y_given = lax.dynamic_index_in_dim(shares, 1 - y, 0, keepdims=False)
    shares = in_order(y == 1, y_kept, swap_y(y_given))
    core_kept = lax.dynamic_index_in_dim(shares, core, 1, keepdims=False)
    core_given = lax.dynamic_index_in_dim(shares, 1 - core, 1, keepdims=False)
    shares = in_order(core == 1, core_kept, swap_core(core_given))
    gathered = spread(shares, "z").transpose(1, 0, 2, 3, 4)
    dev_qkv = gathered[:, :, :, :own_d].reshape(width, 3 * piece)
    small_all = gathered[:, :, :, own_d:].reshape(16, 8 * 3 * piece).astype(full)
    vectors = small_all[:, : 8 * own_d].reshape(16, 8, own_d).transpose(1, 0, 2).reshape(8, width)
    gain_float, bias_float = vectors[:2], vectors[2:]
    up_parts = small_all[:, 8 * own_d : 8 * own_d + hidden_part].reshape(2, 4, 2, hidden_part)
    up_float = lax.dynamic_index_in_dim(
        lax.dynamic_index_in_dim(up_parts, x, 0, keepdims=False), y, 1, keepdims=False
    ).reshape(4 * hidden_part)
    code = small_all[z // 2 * 8, 8 * own_d + hidden_part :][:4]
    length = (code[z % 2] * 128 + code[2 + z % 2]).astype(jnp.int32)

    up_split = w_up.reshape(own_d, 4, 2, hidden_part)
    up_kept = lax.dynamic_index_in_dim(up_split, y, 2, keepdims=False)
    up_given = lax.dynamic_index_in_dim(up_split, 1 - y, 2, keepdims=False)
    up_rows = in_order(y == 1, up_kept, swap_y(up_given)).reshape(2 * own_d, 4 * hidden_part)
    dev_up = lax.all_gather(up_rows, LINE, axis=0, tiled=True)

    corner = [(0, 0), (1, 2), (2, 1), (3, 3)]
    down_rows = lax.ppermute(w_down, ("dp", "head"), corner)
    packed = lax.all_gather(jnp.concatenate([w_out, down_rows]), LINE)
    down_halves = packed[:, own_d:].reshape(2, 4 * hidden_part, width // 2)
    out_line = lax.dynamic_slice_in_dim(packed[:, :own_d], 4 * core, 4)

    cotangent_rows = to_planes(cotangent, z_odd)

    core_rows = plane_gather(token_rows)
    all_rows = jnp.concatenate([core_rows, swap_core(core_rows)])

    first_col = (x * 8 + y * 4 + core * 2) * HD
    query_shift = lax.dynamic_slice_in_dim(bias_float[0], first_col, piece)
    value_shift = lax.dynamic_slice_in_dim(bias_float[1], first_col, piece)
    qkv_shift = jnp.concatenate([query_shift, jnp.zeros((piece,), full), value_shift])
    qkv = (jnp.dot(all_rows, dev_qkv, preferred_element_type=full) + qkv_shift).astype(low)
    out_line = after(out_line.reshape(4, own_d, width // 2), qkv)
    out_plane = spread(out_line, ("y", "head")).reshape(2, 2, 4, own_d, width // 2)
    out_plane = out_plane.transpose(1, 2, 0, 3, 4)
    out_cores = in_order(core == 1, out_plane, swap_core(out_plane))
    out_halves = out_cores.transpose(1, 0, 2, 3, 4, 5).reshape(2, width, width // 2)

    slot = jnp.arange(8, dtype=jnp.int32)
    slots = slot ^ (core * 4 + y * 2 + x)
    slot_core, slot_y, slot_x = slots // 4, slots // 2 % 2, slots % 2
    turn = jnp.arange(2, dtype=jnp.int32)
    from_z = 2 * slot_core[:, None] + (z + turn[None, :]) % 2
    block = (from_z * 2 + slot_y[:, None]) * 2 + slot_x[:, None]
    positions = block[:, :, None] * local_len + jnp.arange(local_len, dtype=jnp.int32)
    bias = jnp.where(positions.reshape(-1, 1) < length, 0.0, NEGATIVE).astype(full)
    attended = attend_heads(slots, qkv, bias)
    returned = lax.all_to_all(attended, PLANE, split_axis=0, concat_axis=0, tiled=True)
    attn_rows = (
        returned.reshape(2, 2, 2, rows, piece).transpose(3, 2, 1, 0, 4).reshape(rows, width)
    )
    projected = halves_dot(attn_rows, out_halves) + bias_float[2]
    first_sum = token_rows.astype(full) + projected
    normed, first_back = jax.vjp(norm_rows, first_sum, gain_float[0], bias_float[3])

    swaps = (swap_x, swap_y, swap_xy)
    normed_low = normed.astype(low)
    normed_parts = [normed_low] + [swap(normed_low) for swap in swaps]
    activ_parts, gelu_backs, ffn_terms = [], [], []
    for part in normed_parts:
        pre_act = jnp.dot(part, dev_up, preferred_element_type=full) + up_float
        activated, gelu_back = jax.vjp(exact_gelu, pre_act)
        activ_parts.append(activated.astype(low))
        gelu_backs.append(gelu_back)
        ffn_terms.append(halves_dot(activ_parts[-1], down_halves))
    ffn_out = ffn_terms[0]
    for swap, term in zip(swaps, ffn_terms[1:]):
        ffn_out = ffn_out + swap(term.astype(low)).astype(full)
    second_sum = normed + ffn_out + bias_float[4]
    result, second_back = jax.vjp(norm_rows, second_sum, gain_float[1], bias_float[5])
    output = from_planes(result.astype(low), z_odd)
    grad_second, gain_grad_two, shift_grad_two = second_back(cotangent_rows.astype(full))
    grad_ffn = grad_second.astype(low)
    shift_grad_down = jnp.sum(grad_ffn.astype(full), axis=0)

    ffn_parts = [grad_ffn] + [swap(grad_ffn) for swap in swaps]
    pre_parts, back_terms = [], []
    for part, gelu_back in zip(ffn_parts, gelu_backs):
        (grad_act,) = gelu_back(halves_dot_back(part, down_halves))
        pre_parts.append(grad_act.astype(low))
        back_terms.append(jnp.dot(pre_parts[-1], dev_up.T, preferred_element_type=full))
    back_sent = [swap(term.astype(low)) for swap, term in zip(swaps, back_terms[1:])]

    ffn_all = jnp.concatenate(ffn_parts)
    activ_all = jnp.concatenate(activ_parts)
    grad_down = jnp.einsum(
        "th,tcd->chd",
        activ_all,
        ffn_all.reshape(4 * rows, 2, width // 2),
        preferred_element_type=full,
    )
    down_total = lax.psum_scatter(
        grad_down.astype(low).reshape(8, hidden_part, width // 2),
        LINE,
        scatter_dimension=0,
        tiled=True,
    ).reshape(hidden_part, width // 2)
    grad_normed = grad_second + back_terms[0]
    for sent in back_sent:
        grad_normed = grad_normed + sent.astype(full)
    share_down = lax.ppermute(down_total, ("dp", "head"), corner).astype(full)

    pre_all = jnp.concatenate(pre_parts)
    normed_all = jnp.concatenate(normed_parts)
    grad_up_shift = jnp.sum(pre_all.astype(full), axis=0)
    grad_up = jnp.dot(normed_all.T, pre_all, preferred_element_type=full)

    grad_first, gain_grad_one, shift_grad_one = first_back(grad_normed)
    grad_proj = grad_first.astype(low)
    shift_grad_out = jnp.sum(grad_proj.astype(full), axis=0)
    grad_attn = halves_dot_back(grad_proj, out_halves).astype(low)
    grad_out = lax.all_to_all(
        grad_attn.reshape(rows, 2, 2, 2, piece).transpose(3, 2, 1, 0, 4).reshape(8, rows, piece),
        PLANE,
        split_axis=0,
        concat_axis=0,
        tiled=True,
    )
    share_up = lax.psum_scatter(grad_up.astype(low), LINE, scatter_dimension=0, tiled=True)
    share_up = share_up.reshape(2, own_d, 4, hidden_part)
    up_home = lax.dynamic_index_in_dim(share_up, y, 0, keepdims=False)
    up_away = lax.dynamic_index_in_dim(share_up, 1 - y, 0, keepdims=False)
    share_up = (
        in_order(y == 1, up_home, swap_y(up_away))
        .transpose(1, 2, 0, 3)
        .reshape(own_d, 8 * hidden_part)
        .astype(full)
    )

    grad_outw = jnp.dot(attn_rows.T, grad_proj, preferred_element_type=full)
    grad_outw = core_sum(grad_outw.reshape(2, 4, 2, own_d, width), core)
    grad_outw = grad_outw.reshape(4, 2, own_d, 2, width // 2).transpose(1, 3, 0, 2, 4)
    out_total = term_sum(grad_outw.reshape(4, 4, own_d, width // 2), ("y", "head"))
    share_out = term_sum(out_total, "z")

    grad_qkv = attend_back(slots, qkv, grad_out, bias)
    column_sums = jnp.sum(grad_qkv.astype(full), axis=0)

    back_terms = jnp.dot(grad_qkv, dev_qkv.T, preferred_element_type=full)
    core_terms = back_terms[: 4 * rows] + swap_core(back_terms[4 * rows :].astype(low)).astype(full)
    core_terms = after(core_terms, out_total)
    grad_rows = after(grad_first + plane_sum(core_terms), down_total)
    grad_tokens = from_planes(grad_rows.astype(low), z_odd).astype(full)

    grad_w = jnp.dot(all_rows.T, grad_qkv, preferred_element_type=full)
    grad_w = grad_w.astype(low).reshape(2, 4, 2, own_d, 3 * piece).transpose(1, 0, 2, 3, 4)
    grad_w = term_sum(grad_w, "z").astype(low)
    sent = jnp.stack([grad_w[..., : 2 * piece], grad_w[..., piece:]], axis=2)
    back = lax.all_to_all(
        sent.reshape(8, own_d, 2 * piece), PLANE, split_axis=0, concat_axis=0, tiled=True
    )
    back = back.reshape(2, 2, 2, own_d, 2, piece).transpose(3, 4, 2, 1, 0, 5)
    back = back.reshape(own_d, 2, 2, 4 * piece)
    share_qkv = jnp.concatenate(
        [
            jnp.where(x == 0, back[:, 0, 0], back[:, 0, 1]),
            jnp.where(x == 0, back[:, 0, 1], back[:, 1, 0]),
            jnp.where(x == 0, back[:, 1, 0], back[:, 1, 1]),
        ],
        axis=1,
    ).astype(full)

    def placed(part):
        return lax.dynamic_update_slice(jnp.zeros((1, width), full), part[None], (0, first_col))

    vector_grads = jnp.concatenate(
        [
            gain_grad_one[None],
            gain_grad_two[None],
            placed(column_sums[:piece]),
            placed(column_sums[2 * piece :]),
            shift_grad_out[None],
            shift_grad_one[None],
            shift_grad_down[None],
            shift_grad_two[None],
        ]
    )
    vector_grads = lax.optimization_barrier(vector_grads)
    vector_grads = vector_grads.reshape(8, 16, own_d).transpose(1, 0, 2).reshape(16, 8 * own_d)
    at_core = (jnp.arange(2) == x)[:, None, None, None]
    at_y = (jnp.arange(2) == y)[None, None, :, None]
    up_grads = jnp.where(at_core & at_y, grad_up_shift.reshape(1, 4, 1, hidden_part), 0.0)
    small_grads = jnp.concatenate([vector_grads, up_grads.reshape(16, hidden_part)], axis=1)
    small_back = exchanged(jnp.repeat(small_grads, 2, axis=0), EVERY)
    small_total = jnp.sum(small_back, axis=0)
    vector_total = small_total[: 8 * own_d].reshape(8, own_d)
    return (
        output,
        grad_tokens,
        share_qkv,
        share_out,
        share_up,
        share_down,
        vector_total[:2],
        vector_total[2:],
        small_total[8 * own_d :],
    )


def fits_planes(mesh):
    return dict(mesh.shape) == {"dp": 2, "blk": 8, "head": 2}


def solution(mesh):
    if fits_planes(mesh):
        body = on_plane
        mesh = jax.sharding.Mesh(mesh.devices.reshape(2, 4, 2, 2), EVERY)
        blk = ("z", "y")
    else:
        body = on_device
        blk = ("blk",)
    token_spec = P("dp", (*blk, "head"), None)
    weight_spec = P(("dp", *blk), "head")
    vector_spec = P(None, ("dp", *blk))
    hidden_spec = P(("dp", *blk))
    return jax.shard_map(
        body,
        mesh=mesh,
        in_specs=(
            token_spec,
            *[weight_spec] * 4,
            vector_spec,
            vector_spec,
            hidden_spec,
            P("dp"),
            token_spec,
        ),
        out_specs=(
            token_spec,
            token_spec,
            *[weight_spec] * 4,
            vector_spec,
            vector_spec,
            hidden_spec,
        ),
        check_vma=False,
    )
```
